256 devices in a mesh: dp: 16 (over x_lo, y, core), blk: 16 (over x_hi, z).
Axes of the slice: x: 4 (x_hi: 2, x_lo: 2; x = x_hi * 2 + x_lo), y: 4, z: 8, core: 2. Of those that a mesh axis runs over, the one named last changes fastest.
Arguments:
- activations: bfloat16 [4096, 14336], P('dp'), may hold values from -6 to 6
- out_grads: bfloat16 [4096, 4096], P('dp'), may hold values from -0.75 to 0.75
- basis_in: bfloat16 [14336, 8192], P('dp', 'blk'), may hold values from -0.046875 to 0.046875
- basis_out: bfloat16 [4096, 4096], P(None, 'blk'), may hold values from -0.09375 to 0.09375
Outputs:
- correction: float32 [4096, 8192], P('dp', 'blk')
The draws below stay inside these ranges and needn't reach their ends.
All inputs are finite; a program needn't handle non-finite values.
Results may differ from the reference program's by a relative error of at most 0.0017.
Values may be sent and summed in bfloat16 or wider, within the bound.
No kernel may reach another device: no remote copies, remote signals or barrier semaphores. Data moves between devices by JAX's collectives and lax.ppermute only.
A program may use at most 128 MiB of HBM per device.

```python
import jax
import jax.numpy as jnp
from jax import lax

D = 4096
FF = 14336
K = 8192
TOK = 128
EXAMPLES = 2
TOKENS = 4096
N_DP = 16


def shard_levels(own_key, extent, pieces, low, largest):
    loudness, own = 1.0, jax.random.fold_in(own_key, 6)
    for position, parts in pieces:
        draws = jnp.exp(jax.random.uniform(jax.random.fold_in(own, position), (parts,), jnp.float32, low / len(pieces), largest / len(pieces)))
        loudness = loudness * jnp.repeat(draws, extent[position] // parts).reshape([-1 if axis == position else 1 for axis in range(len(extent))])
    return loudness


def bell_draw(key, shape, deviation, bound, cuts=(), held_as=jnp.bfloat16):
    result = deviation * jax.random.normal(key, shape, jnp.float32)
    if cuts:
        result = result * shard_levels(key, shape, cuts, -0.22, 0.18)
    return jnp.clip(result, -bound, bound).astype(held_as)


def setup_inputs(seed: int = 0) -> dict:
    streams_of = jax.random.split(jax.random.key(seed), 5)
    activations = bell_draw(streams_of[0], (TOKENS, FF), 1.0, 6.0, ((0, 16),))
    out_grads = bell_draw(streams_of[1], (TOKENS, D), 0.125, 0.75, ((0, 16),))
    basis_in = bell_draw(streams_of[2], (FF, K), FF ** -0.5, 0.046875, ((0, 16), (1, 16)))
    basis_out = bell_draw(streams_of[3], (D, D), D ** -0.5, 0.09375, ((1, 16),))
    return {"activations": activations, "out_grads": out_grads, "basis_in": basis_in, "basis_out": basis_out}


def reference(activations, out_grads, basis_in, basis_out):
    proj_in = jnp.dot(activations, basis_in, preferred_element_type=jnp.float32).astype(jnp.bfloat16)
    proj_out = jnp.dot(out_grads, basis_out, preferred_element_type=jnp.float32).astype(jnp.bfloat16)
    count = EXAMPLES * N_DP
    left = proj_out.reshape(count, TOK, D)
    right = proj_in.reshape(count, TOK, K)

    def add_example(total, pair):
        out_rows, in_rows = pair
        rotated = jnp.dot(out_rows.T, in_rows, preferred_element_type=jnp.float32)
        return total + rotated * rotated, None

    total, unused = lax.scan(add_example, jnp.zeros((D, K), jnp.float32), (left, right))
    return total / jnp.float32(count)
```

```python
import jax
import jax.numpy as jnp
from jax import lax
from jax.experimental import pallas as pl
from jax.experimental.pallas import tpu as pltpu
from jax.sharding import PartitionSpec as P

TOK = 128
EXAMPLES = 2
NX, NY, NC = 2, 4, 2
NH, NZ = 2, 8
SHORT = 384
CHUNKS = ((0, 256), (256, 256))
OWN, LEFT, RIGHT, ACROSS, FAR = (0, 0), (0, 3), (0, 1), (1, 0), (0, 2)
X_LEFT, X_RIGHT, X_FAR = (1, 3), (1, 1), (1, 2)
ORDER = (OWN, LEFT, RIGHT, ACROSS, FAR, X_LEFT, X_RIGHT, X_FAR)


def dp_index(x, y, c):
    return (x * NY + y) * NC + c


def shift(value, dx=0, dy=0, dc=0):
    pairs = [
        (dp_index(x, y, c), dp_index((x + dx) % NX, (y + dy) % NY, (c + dc) % NC))
        for x in range(NX)
        for y in range(NY)
        for c in range(NC)
    ]
    return lax.ppermute(value, "dp", pairs)


def dot(a, b):
    return jnp.dot(a, b, preferred_element_type=jnp.float32)


def squares_kernel(where_ref, out_ref_rows, *refs):
    in_rows, total_ref = refs[:-1], refs[-1]
    half = total_ref.shape[0] // 2
    for part in range(2):
        rows = pl.ds(part * half, half)
        total = None
        for k, block in enumerate(in_rows):
            at = where_ref[k]
            for example in range(EXAMPLES):
                tokens = pl.ds(example * TOK, TOK)
                rotated = dot(out_ref_rows[at, rows, tokens], block[tokens, :])
                squared = rotated * rotated
                total = squared if total is None else total + squared
        total_ref[rows, :] = total


def sums_of_squares(where, out_rows, in_rows):
    rows, width = out_rows.shape[1], in_rows[0].shape[1]
    vmem = pl.BlockSpec(memory_space=pltpu.VMEM)
    return pl.pallas_call(
        squares_kernel,
        out_shape=jax.ShapeDtypeStruct((rows, width), jnp.float32),
        in_specs=[pl.BlockSpec(memory_space=pltpu.SMEM)] + [vmem] * (1 + len(in_rows)),
        out_specs=vmem,
        compiler_params=pltpu.CompilerParams(vmem_limit_bytes=32 * 1024 * 1024),
        cost_estimate=pl.CostEstimate(
            flops=2 * rows * width * len(in_rows) * EXAMPLES * TOK,
            bytes_accessed=out_rows.size * 2 + rows * width * 4,
            transcendentals=0,
        ),
    )(where, out_rows, *in_rows)


def on_device(activations, out_grads, basis_in, basis_out):
    d, b = lax.axis_index("dp"), lax.axis_index("blk")
    core, y, x = d % NC, (d // NC) % NY, d // (NC * NY)
    scale = 1.0 / float(EXAMPLES * NX * NY * NC)
    depth = basis_in.shape[0]
    place = [((x + dx) % NX) * NY + (y + dy) % NY for dx, dy in ORDER]

    block = dot(out_grads, basis_out).astype(jnp.bfloat16).T
    pairs = []
    for sx in range(NX):
        for sy in range(NY):
            for sc in range(NC):
                for tx in range(NX):
                    for ty in range(NY):
                        for tc in range(NC):
                            source = dp_index(sx, sy, sc) * NH * NZ + dp_index(tx, ty, tc)
                            target = dp_index(tx, ty, sc) * NH * NZ + tc * NZ + sx * NY + sy
                            pairs.append((source, target))
    block = lax.ppermute(block, ("dp", "blk"), pairs)
    other = lax.ppermute(
        block, "blk", [(h * NZ + z, (1 - h) * NZ + z) for h in range(NH) for z in range(NZ)]
    )
    mine = (b // NZ) == core
    block = jnp.concatenate([jnp.where(mine, block, other), jnp.where(mine, other, block)], 0)
    out_rows = lax.all_gather(
        block,
        "blk",
        axis=0,
        axis_index_groups=[[h * NZ + z for z in range(NZ)] for h in range(NH)],
    )
    where = jnp.stack(place).astype(jnp.int32)

    def columns(parity):
        return jnp.stack(
            [
                lax.dynamic_slice_in_dim(activations, (p * NC + parity) * depth, depth, 1)
                for p in place
            ]
        )

    rows = jnp.concatenate([columns(core), shift(columns(1 - core), dc=1)], 1)
    a = dict(zip(ORDER, [rows[k] for k in range(len(ORDER))]))
    tokens = activations.shape[0]

    results = []
    for start, width in CHUNKS:
        own = lax.slice_in_dim(basis_in, start, start + width, axis=1)
        left, right, across = shift(own, dy=1), shift(own, dy=3), shift(own, dx=1)
        total = dot(a[OWN], own) + dot(a[LEFT], left) + dot(a[RIGHT], right)
        total = total + dot(a[ACROSS], across)
        up = shift(jnp.concatenate([across[:SHORT], left[:SHORT]], 0), dy=1)
        down = shift(jnp.concatenate([across[:SHORT], right[SHORT:]], 0), dy=3)
        over = shift(jnp.concatenate([left[SHORT:], right[SHORT:]], 0), dx=1)
        long = depth - SHORT
        far = jnp.concatenate([up[SHORT:], down[SHORT:]], 0)
        x_left = jnp.concatenate([up[:SHORT], over[:long]], 0)
        x_right = jnp.concatenate([down[:SHORT], over[long:]], 0)
        total = total + dot(a[FAR], far) + dot(a[X_LEFT], x_left) + dot(a[X_RIGHT], x_right)
        x_far = jnp.concatenate(
            [shift(x_left[:SHORT], dy=1), shift(x_right[SHORT:], dy=3)], 0
        )
        total = total + dot(a[X_FAR], x_far)
        proj_in = (total[:tokens] + shift(total[tokens:], dc=1)).astype(jnp.bfloat16)

        p_left, p_right, p_far = shift(proj_in, dy=1), shift(proj_in, dy=3), shift(proj_in, dy=2)
        p_across = shift(proj_in, dx=1)
        px_left, px_right = shift(p_across, dy=1), shift(p_across, dy=3)
        px_far = shift(p_far, dx=1)
        sums = sums_of_squares(
            where,
            out_rows,
            (proj_in, p_left, p_right, p_across, p_far, px_left, px_right, px_far),
        )
        half = sums.shape[0] // 2
        results.append((sums[:half] + shift(sums[half:], dc=1)) * jnp.float32(scale))
    return jnp.concatenate(results, 1)


def solution(mesh):
    return jax.shard_map(
        on_device,
        mesh=mesh,
        in_specs=(P("dp", None), P("dp", None), P("dp", "blk"), P(None, "blk")),
        out_specs=P("dp", "blk"),
        check_vma=False,
    )
```

```python
import jax
import jax.numpy as jnp
from jax import lax
from jax.experimental import pallas as pl
from jax.experimental.pallas import tpu as pltpu
from jax.sharding import PartitionSpec as P

TOK = 128
EXAMPLES = 2
NX, NY, NC = 2, 4, 2
NH, NZ = 2, 8
SHORT = 384
SPLIT = 3
CHUNKS = ((0, 512),)
FACTOR = 32.0
VMEM = 18 * 1024 * 1024
BLOCKS = ((0, 0), (0, 1), (3, 0), (3, 1), (1, 0), (1, 1), (2, 0), (2, 1))
ORDER = ((0, 0), (0, 3), (0, 1), (1, 0), (0, 2), (1, 3), (1, 1), (1, 2))


def index(x, y, z, c):
    return ((x % NX * NY + y) * NC + c) * NH * NZ + x // NX * NZ + z


def shift(value, dx=0, dy=0, dz=0, dc=0):
    size = NX * NH
    pairs = [
        (index(x, y, z, c), index((x + dx) % size, (y + dy) % NY, (z + dz) % NZ, (c + dc) % NC))
        for x in range(size)
        for y in range(NY)
        for z in range(NZ)
        for c in range(NC)
    ]
    return lax.ppermute(value, ("dp", "blk"), pairs)


def swap(value, dy=0):
    pairs = [
        (index(x, y, z, c), index(x ^ 1, (y + dy) % NY, z, c))
        for x in range(NX * NH)
        for y in range(NY)
        for z in range(NZ)
        for c in range(NC)
    ]
    return lax.ppermute(value, ("dp", "blk"), pairs)


def dot(a, b):
    return jnp.dot(a, b, preferred_element_type=jnp.float32)


def space(kind):
    return pl.BlockSpec(memory_space=kind)


def pieces_kernel(columns_ref, source, *refs):
    outs, semaphore = refs[:-1], refs[-1]
    copies = []
    for part, count in ((0, SPLIT), (SPLIT, len(BLOCKS) - 2 * SPLIT)):
        for example in range(EXAMPLES):
            out = outs[(2 if part else 0) + example]
            for i in range(count):
                column = pl.multiple_of(columns_ref[part + i], 128)
                copies.append(
                    pltpu.make_async_copy(
                        source.at[pl.ds(example * TOK, TOK), pl.ds(column, out.shape[2])],
                        out.at[i],
                        semaphore.at[len(copies)],
                    )
                )
    for copy in copies:
        copy.start()
    for copy in copies:
        copy.wait()


def pieces(columns, activations, depth):
    rest = len(BLOCKS) - 2 * SPLIT
    kinds = [SPLIT, SPLIT, rest, rest]
    return pl.pallas_call(
        pieces_kernel,
        out_shape=[jax.ShapeDtypeStruct((n, TOK, depth), activations.dtype) for n in kinds],
        in_specs=[space(pltpu.SMEM), space(pl.ANY)],
        out_specs=[space(pl.ANY)] * 4,
        scratch_shapes=[pltpu.SemaphoreType.DMA((sum(kinds),))],
        cost_estimate=pl.CostEstimate(flops=0, bytes_accessed=2**23, transcendentals=0),
    )(columns, activations)


def times_basis(block, panels, blocks, columns):
    total = None
    for k in range(len(BLOCKS)):
        a = block(k)
        if k < len(BLOCKS) - 2:
            term = dot(a, panels[k][:, columns])
        else:
            short, long = panels[2 * k - 6], panels[2 * k - 5]
            term = dot(a[:, :SHORT], short[:, columns]) + dot(a[:, SHORT:], long[:, columns])
        total = term if total is None else total + term
    return total


TILE = 256


def theirs_kernel(start, parity_ref, *refs):
    near, rest, panels, out = refs[:4], refs[4:6], refs[6:-1], refs[-1]

    def work(low, high):
        def block(k):
            pair, at = (low, k) if k < SPLIT else (high, k - SPLIT) if k < 2 * SPLIT else (rest, k - 2 * SPLIT)
            return jnp.concatenate([pair[0][at], pair[1][at]], 0)

        @pl.loop(0, out.shape[1] // TILE)
        def _(n):
            offset = pl.multiple_of(n * TILE, TILE)
            out[:, pl.ds(offset, TILE)] = times_basis(
                block, panels, BLOCKS, pl.ds(pl.multiple_of(start + offset, TILE), TILE)
            )

    @pl.when(parity_ref[0] == 0)
    def _():
        work(near[:2], near[2:])

    @pl.when(parity_ref[0] != 0)
    def _():
        work(near[2:], near[:2])


def theirs(parity, near, rest, panels, start, width):
    tokens = EXAMPLES * TOK
    return pl.pallas_call(
        lambda *refs: theirs_kernel(start, *refs),
        out_shape=jax.ShapeDtypeStruct((tokens, width), jnp.float32),
        in_specs=[space(pltpu.SMEM)] + [space(pltpu.VMEM)] * (6 + len(panels)),
        out_specs=space(pltpu.VMEM),
        compiler_params=pltpu.CompilerParams(vmem_limit_bytes=VMEM),
        cost_estimate=pl.CostEstimate(
            flops=2 * tokens * width * 7168, bytes_accessed=2**22, transcendentals=0
        ),
    )(parity, *near, *rest, *panels)


def ours_kernel(start, columns_ref, source, *refs):
    panels, out, rows, semaphore = refs[:-3], refs[-3], refs[-2], refs[-1]
    copies = [
        pltpu.make_async_copy(
            source.at[:, pl.ds(pl.multiple_of(columns_ref[k], 128), rows.shape[2])],
            rows.at[k],
            semaphore.at[k],
        )
        for k in range(len(BLOCKS))
    ]
    for copy in copies:
        copy.start()
    for copy in copies:
        copy.wait()

    @pl.loop(0, out.shape[1] // TILE)
    def _(n):
        offset = pl.multiple_of(n * TILE, TILE)
        out[:, pl.ds(offset, TILE)] = times_basis(
            lambda k: rows[k], panels, BLOCKS, pl.ds(pl.multiple_of(start + offset, TILE), TILE)
        )


def ours(columns, activations, panels, start, width):
    tokens, depth = activations.shape[0], panels[0].shape[0]
    return pl.pallas_call(
        lambda *refs: ours_kernel(start, *refs),
        out_shape=jax.ShapeDtypeStruct((tokens, width), jnp.float32),
        in_specs=[space(pltpu.SMEM), space(pl.ANY)] + [space(pltpu.VMEM)] * len(panels),
        out_specs=space(pltpu.VMEM),
        scratch_shapes=[
            pltpu.VMEM((len(BLOCKS), tokens, depth), activations.dtype),
            pltpu.SemaphoreType.DMA((len(BLOCKS),)),
        ],
        compiler_params=pltpu.CompilerParams(vmem_limit_bytes=VMEM),
        cost_estimate=pl.CostEstimate(
            flops=2 * tokens * width * 7168, bytes_accessed=2**22, transcendentals=0
        ),
    )(columns, activations, *panels)


def squares_kernel(where_ref, out_rows, *refs):
    in_rows, total_ref = refs[:-1], refs[-1]
    half = total_ref.shape[0] // 2

    @pl.loop(0, total_ref.shape[1] // TILE)
    def _(n):
        columns = pl.ds(pl.multiple_of(n * TILE, TILE), TILE)
        for part in range(2):
            rows = pl.ds(part * half, half)
            total = None
            for k, block in enumerate(in_rows):
                at = where_ref[k]
                for example in range(EXAMPLES):
                    tokens = pl.ds(example * TOK, TOK)
                    rotated = dot(out_rows[at, rows, tokens], block[tokens, columns])
                    squared = rotated * rotated
                    total = squared if total is None else total + squared
            total_ref[rows, columns] = total


def sums_of_squares(where, out_rows, in_rows):
    rows, width = out_rows.shape[1], in_rows[0].shape[1]
    return pl.pallas_call(
        squares_kernel,
        out_shape=jax.ShapeDtypeStruct((rows, width), jnp.float32),
        in_specs=[space(pltpu.SMEM)] + [space(pltpu.VMEM)] * (1 + len(in_rows)),
        out_specs=space(pltpu.VMEM),
        compiler_params=pltpu.CompilerParams(vmem_limit_bytes=VMEM),
        cost_estimate=pl.CostEstimate(
            flops=2 * rows * width * len(in_rows) * EXAMPLES * TOK,
            bytes_accessed=out_rows.size * 2 + rows * width * 4,
            transcendentals=0,
        ),
    )(where, out_rows, *in_rows)


def transposed(block):
    pairs = []
    for sx in range(NX):
        for sy in range(NY):
            for sc in range(NC):
                for t in range(NX * NY * NC):
                    source = ((sx * NY + sy) * NC + sc) * NH * NZ + t
                    target = (t // NC * NC + sc) * NH * NZ + t % NC * NZ + sx * NY + sy
                    pairs.append((source, target))
    return lax.ppermute(block, ("dp", "blk"), pairs)


def on_device(activations, out_grads, basis_in, basis_out):
    d, b = lax.axis_index("dp"), lax.axis_index("blk")
    core, y, x = d % NC, (d // NC) % NY, d // (NC * NY)
    parity = b % 2
    scale = 1.0 / float(EXAMPLES * NX * NY * NC)
    depth = basis_in.shape[0]
    spots = [((y + dy) % NY) * NC + (core + dc) % NC for dy, dc in BLOCKS]
    half = len(BLOCKS)

    left, right = shift(basis_in, dy=1), shift(basis_in, dy=3)
    own_other = shift(basis_in, dc=1)

    block = transposed(dot(out_grads, basis_out).astype(jnp.bfloat16).T)
    other = shift(block, dx=NX)
    mine = (b // NZ) == core
    block = jnp.concatenate([jnp.where(mine, block, other), jnp.where(mine, other, block)], 0)
    out_rows = lax.all_gather(
        block,
        "blk",
        axis=0,
        axis_index_groups=[[h * NZ + z for z in range(NZ)] for h in range(NH)],
    )
    where = jnp.stack([((x + dx) % NX) * NY + (y + dy) % NY for dx, dy in ORDER]).astype(jnp.int32)

    table = jnp.stack(spots)
    give = jnp.concatenate(
        [lax.dynamic_slice_in_dim(table, parity * SPLIT, SPLIT), table[2 * SPLIT :]]
    )
    give = ((half * (1 - x) + give) * depth).astype(jnp.int32)
    near0, near1, rest0, rest1 = pieces(give, activations, depth)
    near0, near1 = shift(near0, dx=3), shift(near1, dx=1)
    rest0, rest1 = shift(rest0, dx=3), shift(rest1, dx=1)
    away0, away1 = shift(near0, dz=NZ - 1), shift(near1, dz=1)

    far_short, far_long = shift(left[:SHORT], dy=1), shift(right[SHORT:], dy=3)
    panels = [basis_in, own_other, left, shift(left, dc=1), right, shift(right, dc=1)]
    panels += [far_short, far_long, shift(far_short, dc=1), shift(far_long, dc=1)]
    keep = ((half * x + table) * depth).astype(jnp.int32)
    parity = parity.reshape(1).astype(jnp.int32)

    results = []
    for start, width in CHUNKS:
        partial = theirs(parity, (near0, near1, away0, away1), (rest0, rest1), panels, start, width)
        arrived = swap((partial * FACTOR).astype(jnp.float16)).astype(jnp.float32) * (1.0 / FACTOR)
        total = ours(keep, activations, panels, start, width)
        proj_in = (total + arrived).astype(jnp.bfloat16)

        p_left, p_right, p_far = shift(proj_in, dy=1), shift(proj_in, dy=3), shift(proj_in, dy=2)
        p_across = swap(proj_in)
        px_left, px_right = shift(p_across, dy=1), shift(p_across, dy=3)
        px_far = swap(p_far)
        sums = sums_of_squares(
            where,
            out_rows,
            (proj_in, p_left, p_right, p_across, p_far, px_left, px_right, px_far),
        )
        rows = sums.shape[0] // 2
        results.append((sums[:rows] + shift(sums[rows:], dc=1)) * jnp.float32(scale))
    return jnp.concatenate(results, 1) if len(results) > 1 else results[0]


def solution(mesh):
    return jax.shard_map(
        on_device,
        mesh=mesh,
        in_specs=(P("dp", None), P("dp", None), P("dp", "blk"), P(None, "blk")),
        out_specs=P("dp", "blk"),
        check_vma=False,
    )
```

```python
import jax
import jax.numpy as jnp
from jax import lax
from jax.experimental import pallas as pl
from jax.experimental.pallas import tpu as pltpu
from jax.sharding import PartitionSpec as P

TOK = 128
EXAMPLES = 2
NX, NY, NC = 2, 4, 2
NH, NZ = 2, 8
SPLIT = 2
FACTOR = 32.0
VMEM = 60 * 1024 * 1024
BLOCKS = ((0, 0), (0, 1), (3, 0), (3, 1), (1, 0), (1, 1), (2, 0), (2, 1))
ORDER = ((0, 0), (0, 3), (0, 1), (1, 0), (0, 2), (1, 3), (1, 1), (1, 2))


def index(x, y, z, c):
    return ((x % NX * NY + y) * NC + c) * NH * NZ + x // NX * NZ + z


def shift(value, dx=0, dy=0, dz=0, dc=0):
    size = NX * NH
    pairs = [
        (index(x, y, z, c), index((x + dx) % size, (y + dy) % NY, (z + dz) % NZ, (c + dc) % NC))
        for x in range(size)
        for y in range(NY)
        for z in range(NZ)
        for c in range(NC)
    ]
    return lax.ppermute(value, ("dp", "blk"), pairs)


def by_core(value, dx=0, dy=0, dz=0):
    size = NX * NH
    pairs = []
    for x in range(size):
        for y in range(NY):
            for z in range(NZ):
                for c, way in ((0, 1), (1, -1)):
                    target = ((x + way * dx) % size, (y + way * dy) % NY, (z + way * dz) % NZ, c)
                    pairs.append((index(x, y, z, c), index(*target)))
    return lax.ppermute(value, ("dp", "blk"), pairs)


def swap(value, dy=0):
    pairs = [
        (index(x, y, z, c), index(x ^ 1, (y + dy) % NY, z, c))
        for x in range(NX * NH)
        for y in range(NY)
        for z in range(NZ)
        for c in range(NC)
    ]
    return lax.ppermute(value, ("dp", "blk"), pairs)


def dot(a, b):
    return jnp.dot(a, b, preferred_element_type=jnp.float32)


def space(kind):
    return pl.BlockSpec(memory_space=kind)


def pieces_kernel(columns_ref, source, near, rest, held, arrived, left):
    moves = []
    for k in range(held.shape[0]):
        column = pl.multiple_of(columns_ref[k], 128)
        out = near.at[k] if k < SPLIT else rest.at[k - SPLIT]
        moves.append(
            (
                pltpu.make_async_copy(
                    source.at[:, pl.ds(column, held.shape[2])], held.at[k], arrived.at[k]
                ),
                pltpu.make_async_copy(held.at[k], out, left.at[k]),
            )
        )
    for get, put in moves:
        get.start()
    for get, put in moves:
        get.wait()
        put.start()
    for get, put in moves:
        put.wait()


def pieces(columns, activations, depth):
    tokens, count = activations.shape[0], len(BLOCKS) - SPLIT
    return pl.pallas_call(
        pieces_kernel,
        out_shape=[
            jax.ShapeDtypeStruct((n, tokens, depth), activations.dtype)
            for n in (SPLIT, count - SPLIT)
        ],
        in_specs=[space(pltpu.SMEM), space(pltpu.HBM)],
        out_specs=[space(pltpu.HBM)] * 2,
        scratch_shapes=[
            pltpu.VMEM((count, tokens, depth), activations.dtype),
            pltpu.SemaphoreType.DMA((count,)),
            pltpu.SemaphoreType.DMA((count,)),
        ],
        compiler_params=pltpu.CompilerParams(vmem_limit_bytes=VMEM),
        cost_estimate=pl.CostEstimate(flops=0, bytes_accessed=2**23, transcendentals=0),
    )(columns, activations)


def product_kernel(moves, layout, *refs):
    table, sources, refs = refs[0], refs[1 : 1 + layout[0]], refs[1 + layout[0] :]
    parts, refs = refs[: sum(layout[1])], refs[sum(layout[1]) :]
    before, (out, rows, panels, semaphore) = refs[:-4], refs[-4:]
    pairs = moves(table, sources, rows)
    for_rows = [pltpu.make_async_copy(*pair, semaphore.at[n]) for n, pair in enumerate(pairs)]
    for_panels, at = [], 0
    for k, count in enumerate(layout[1]):
        filled, copies = 0, []
        for part in parts[at : at + count]:
            target = panels.at[k, pl.ds(filled, part.shape[0])]
            number = len(pairs) + at + len(copies)
            copies.append(pltpu.make_async_copy(part, target, semaphore.at[number]))
            filled += part.shape[0]
        at += count
        for_panels.append(copies)
    for copy in for_rows + sum(for_panels, []):
        copy.start()
    for copy in for_rows:
        copy.wait()
    for k, copies in enumerate(for_panels):
        for copy in copies:
            copy.wait()
        term = dot(rows[k], panels[k])
        if k:
            out[...] += term
        else:
            out[...] = before[0][...] + term if before else term


def product(moves, count, table, sources, panels, before=None):
    tokens, blocks = EXAMPLES * TOK, len(panels)
    depth, width = panels[0][0].shape[0] if len(panels[0]) == 1 else sum(
        part.shape[0] for part in panels[0]
    ), panels[0][0].shape[1]
    parts = sum(panels, [])
    layout = (len(sources), [len(panel) for panel in panels])
    extra = [] if before is None else [before]
    return pl.pallas_call(
        lambda *refs: product_kernel(moves, layout, *refs),
        out_shape=jax.ShapeDtypeStruct((tokens, width), jnp.float32),
        in_specs=[space(pltpu.SMEM)]
        + [space(pl.ANY)] * (len(sources) + len(parts))
        + [space(pltpu.VMEM)] * len(extra),
        out_specs=space(pltpu.VMEM),
        scratch_shapes=[
            pltpu.VMEM((blocks, tokens, depth), jnp.bfloat16),
            pltpu.VMEM((blocks, depth, width), jnp.bfloat16),
            pltpu.SemaphoreType.DMA((count + len(parts),)),
        ],
        compiler_params=pltpu.CompilerParams(vmem_limit_bytes=VMEM),
        cost_estimate=pl.CostEstimate(
            flops=2 * tokens * width * blocks * depth, bytes_accessed=2**22, transcendentals=0
        ),
    )(table, *sources, *parts, *extra)


def near_moves(table, sources, rows):
    return [
        (source, rows.at[pl.ds(start * SPLIT, SPLIT)])
        for start, source in zip((table[0], 1 - table[0]), sources)
    ]


def rest_moves(table, sources, rows):
    return [(sources[0], rows)]


def own_moves(table, sources, rows):
    return [
        (sources[0].at[:, pl.ds(pl.multiple_of(table[k], 128), rows.shape[2])], rows.at[k])
        for k in range(rows.shape[0])
    ]


def squares_kernel(where_ref, out_rows, *refs):
    blocks = (len(refs) - 4)
    in_rows, (total_ref, outer, inner, semaphore) = refs[:-4], refs[-4:]
    copies = [
        (
            pltpu.make_async_copy(out_rows.at[where_ref[k]], outer.at[k], semaphore.at[2 * k]),
            pltpu.make_async_copy(in_rows[k], inner.at[k], semaphore.at[2 * k + 1]),
        )
        for k in range(blocks)
    ]
    for pair in copies:
        pair[0].start()
        pair[1].start()
    for pair in copies:
        pair[0].wait()
        pair[1].wait()
    half = total_ref.shape[0] // 2

    @pl.loop(0, total_ref.shape[1] // TILE)
    def _(n):
        columns = pl.ds(pl.multiple_of(n * TILE, TILE), TILE)
        for part in range(2):
            rows = pl.ds(part * half, half)
            total = None
            for k in range(blocks):
                for example in range(EXAMPLES):
                    tokens = pl.ds(example * TOK, TOK)
                    rotated = dot(outer[k, rows, tokens], inner[k, tokens, columns])
                    squared = rotated * rotated
                    total = squared if total is None else total + squared
            total_ref[rows, columns] = total


TILE = 256


def sums_of_squares(where, out_rows, in_rows):
    rows, tokens = out_rows.shape[1:]
    width, blocks = in_rows[0].shape[1], len(in_rows)
    return pl.pallas_call(
        squares_kernel,
        out_shape=jax.ShapeDtypeStruct((rows, width), jnp.float32),
        in_specs=[space(pltpu.SMEM)] + [space(pl.ANY)] * (1 + blocks),
        out_specs=space(pltpu.VMEM),
        scratch_shapes=[
            pltpu.VMEM((blocks, rows, tokens), jnp.bfloat16),
            pltpu.VMEM((blocks, tokens, width), jnp.bfloat16),
            pltpu.SemaphoreType.DMA((2 * blocks,)),
        ],
        compiler_params=pltpu.CompilerParams(vmem_limit_bytes=VMEM),
        cost_estimate=pl.CostEstimate(
            flops=2 * rows * width * blocks * tokens,
            bytes_accessed=out_rows.size * 2 + rows * width * 4,
            transcendentals=0,
        ),
    )(where, out_rows, *in_rows)


def transposed(block):
    pairs = []
    for sx in range(NX):
        for sy in range(NY):
            for sc in range(NC):
                for t in range(NX * NY * NC):
                    source = ((sx * NY + sy) * NC + sc) * NH * NZ + t
                    target = (t // NC * NC + sc) * NH * NZ + t % NC * NZ + sx * NY + sy
                    pairs.append((source, target))
    return lax.ppermute(block, ("dp", "blk"), pairs)


def on_device(activations, out_grads, basis_in, basis_out):
    d, b = lax.axis_index("dp"), lax.axis_index("blk")
    core, y, x = d % NC, (d // NC) % NY, d // (NC * NY)
    parity = b % 2
    scale = 1.0 / float(EXAMPLES * NX * NY * NC)
    depth = basis_in.shape[0]
    spots = [((y + dy) % NY) * NC + (core + dc) % NC for dy, dc in BLOCKS]
    half = len(BLOCKS)

    table = jnp.stack(spots)
    give = jnp.concatenate(
        [lax.dynamic_slice_in_dim(table, parity * SPLIT, SPLIT), table[2 * SPLIT :]]
    )
    give = ((half * (1 - x) + give) * depth).astype(jnp.int32)
    keep = ((half * x + table) * depth).astype(jnp.int32)
    near, rest = pieces(give, activations, depth)
    left, right = shift(basis_in, dy=1), shift(basis_in, dy=3)
    near, own_other = by_core(near, dx=1), shift(basis_in, dc=1)
    block = transposed(dot(out_grads, basis_out).astype(jnp.bfloat16).T)

    near, left, right, rest, block, own_other = lax.optimization_barrier(
        (near, left, right, rest, block, own_other)
    )
    far = by_core(jnp.where(core == 0, left, right), dy=1)
    rest, away = by_core(rest, dx=1), by_core(near, dz=1)
    left_other, right_other = shift(left, dc=1), shift(right, dc=1)

    other = shift(block, dx=NX)
    mine = (b // NZ) == core
    block = jnp.concatenate([jnp.where(mine, block, other), jnp.where(mine, other, block)], 0)
    out_rows = lax.all_gather(
        block,
        "blk",
        axis=0,
        axis_index_groups=[[h * NZ + z for z in range(NZ)] for h in range(NH)],
    )
    where = jnp.stack([((x + dx) % NX) * NY + (y + dy) % NY for dx, dy in ORDER]).astype(jnp.int32)

    panels = [basis_in, own_other, left, left_other, right, right_other, far, shift(far, dc=1)]
    panels = [[panel] for panel in panels]
    parity = parity.reshape(1).astype(jnp.int32)
    partial = product(near_moves, 2, parity, (near, away), panels[: 2 * SPLIT])
    partial = product(rest_moves, 1, parity, (rest,), panels[2 * SPLIT :], partial)
    arrived = swap((partial * FACTOR).astype(jnp.float16))
    total = product(own_moves, len(BLOCKS), keep, (activations,), panels)
    proj_in = (total + arrived.astype(jnp.float32) * (1.0 / FACTOR)).astype(jnp.bfloat16)

    p_left, p_right, p_far = shift(proj_in, dy=1), shift(proj_in, dy=3), shift(proj_in, dy=2)
    p_across = swap(proj_in)
    px_left, px_right = shift(p_across, dy=1), shift(p_across, dy=3)
    px_far = swap(p_far)
    sums = sums_of_squares(
        where,
        out_rows,
        (proj_in, p_left, p_right, p_across, p_far, px_left, px_right, px_far),
    )
    rows = sums.shape[0] // 2
    return (sums[:rows] + shift(sums[rows:], dc=1)) * jnp.float32(scale)


def solution(mesh):
    return jax.shard_map(
        on_device,
        mesh=mesh,
        in_specs=(P("dp", None), P("dp", None), P("dp", "blk"), P(None, "blk")),
        out_specs=P("dp", "blk"),
        check_vma=False,
    )
```

```python
import jax
import jax.numpy as jnp
from jax import lax
from jax.experimental import pallas as pl
from jax.experimental.pallas import tpu as pltpu
from jax.sharding import PartitionSpec as P

TOK = 128
EXAMPLES = 2
NX, NY, NC = 2, 4, 2
NH, NZ = 2, 8
SPLIT = 2
FACTOR = 32.0
VMEM = 60 * 1024 * 1024
FOLLOWED = 6 * 10**9
TAIL_VMEM = 16 * 1024 * 1024
BLOCKS = ((0, 0), (0, 1), (3, 0), (3, 1), (1, 0), (1, 1), (2, 0), (2, 1))
ORDER = ((0, 0), (0, 3), (0, 1), (1, 0), (0, 2), (1, 3), (1, 1), (1, 2))


def index(x, y, z, c):
    return ((x % NX * NY + y) * NC + c) * NH * NZ + x // NX * NZ + z


def shift(value, dx=0, dy=0, dz=0, dc=0):
    size = NX * NH
    pairs = [
        (index(x, y, z, c), index((x + dx) % size, (y + dy) % NY, (z + dz) % NZ, (c + dc) % NC))
        for x in range(size)
        for y in range(NY)
        for z in range(NZ)
        for c in range(NC)
    ]
    return lax.ppermute(value, ("dp", "blk"), pairs)


def by_core(value, dx=0, dy=0, dz=0):
    size = NX * NH
    pairs = []
    for x in range(size):
        for y in range(NY):
            for z in range(NZ):
                for c, way in ((0, 1), (1, -1)):
                    target = ((x + way * dx) % size, (y + way * dy) % NY, (z + way * dz) % NZ, c)
                    pairs.append((index(x, y, z, c), index(*target)))
    return lax.ppermute(value, ("dp", "blk"), pairs)


def swap(value, dy=0):
    pairs = [
        (index(x, y, z, c), index(x ^ 1, (y + dy) % NY, z, c))
        for x in range(NX * NH)
        for y in range(NY)
        for z in range(NZ)
        for c in range(NC)
    ]
    return lax.ppermute(value, ("dp", "blk"), pairs)


def dot(a, b):
    return jnp.dot(a, b, preferred_element_type=jnp.float32)


def space(kind):
    return pl.BlockSpec(memory_space=kind)


def pieces_kernel(columns_ref, source, out, held, arrived, left):
    moves = []
    for k in range(held.shape[0]):
        column = pl.multiple_of(columns_ref[k], 128)
        get = source.at[:, pl.ds(column, held.shape[2])]
        moves.append(
            (
                pltpu.make_async_copy(get, held.at[k], arrived.at[k]),
                pltpu.make_async_copy(held.at[k], out.at[k], left.at[k]),
            )
        )
    for get, put in moves:
        get.start()
    for get, put in moves:
        get.wait()
        put.start()
    for get, put in moves:
        put.wait()


def pieces(columns, activations, depth):
    tokens, count = activations.shape[0], columns.shape[0]
    shape = (count, tokens, depth)
    return pl.pallas_call(
        pieces_kernel,
        out_shape=jax.ShapeDtypeStruct(shape, activations.dtype),
        in_specs=[space(pltpu.SMEM), space(pltpu.HBM)],
        out_specs=space(pltpu.HBM),
        scratch_shapes=[
            pltpu.VMEM(shape, activations.dtype),
            pltpu.SemaphoreType.DMA((count,)),
            pltpu.SemaphoreType.DMA((count,)),
        ],
        compiler_params=pltpu.CompilerParams(vmem_limit_bytes=VMEM),
        cost_estimate=pl.CostEstimate(flops=0, bytes_accessed=2**22, transcendentals=0),
    )(columns, activations)


def product_kernel(moves, layout, *refs):
    table, sources, refs = refs[0], refs[1 : 1 + layout[0]], refs[1 + layout[0] :]
    parts, refs = refs[: sum(layout[1])], refs[sum(layout[1]) :]
    before, (out, rows, panels, semaphore) = refs[:-4], refs[-4:]
    pairs = moves(table, sources, rows)
    for_rows = [pltpu.make_async_copy(*pair, semaphore.at[n]) for n, pair in enumerate(pairs)]
    for_panels, at = [], 0
    for k, count in enumerate(layout[1]):
        filled, copies = 0, []
        for part in parts[at : at + count]:
            target = panels.at[k, pl.ds(filled, part.shape[0])]
            number = len(pairs) + at + len(copies)
            copies.append(pltpu.make_async_copy(part, target, semaphore.at[number]))
            filled += part.shape[0]
        at += count
        for_panels.append(copies)
    for copy in for_rows + sum(for_panels, []):
        copy.start()
    for copy in for_rows:
        copy.wait()
    for k, copies in enumerate(for_panels):
        for copy in copies:
            copy.wait()
        term = dot(rows[k], panels[k])
        if k:
            out[...] += term
        else:
            out[...] = before[0][...] + term if before else term


def product(moves, count, table, sources, panels, before=None, followed_by=0):
    tokens, blocks = EXAMPLES * TOK, len(panels)
    depth, width = panels[0][0].shape[0] if len(panels[0]) == 1 else sum(
        part.shape[0] for part in panels[0]
    ), panels[0][0].shape[1]
    parts = sum(panels, [])
    layout = (len(sources), [len(panel) for panel in panels])
    extra = [] if before is None else [before]
    return pl.pallas_call(
        lambda *refs: product_kernel(moves, layout, *refs),
        out_shape=jax.ShapeDtypeStruct((tokens, width), jnp.float32),
        in_specs=[space(pltpu.SMEM)]
        + [space(pl.ANY)] * (len(sources) + len(parts))
        + [space(pltpu.VMEM)] * len(extra),
        out_specs=space(pltpu.VMEM),
        scratch_shapes=[
            pltpu.VMEM((blocks, tokens, depth), jnp.bfloat16),
            pltpu.VMEM((blocks, depth, width), jnp.bfloat16),
            pltpu.SemaphoreType.DMA((count + len(parts),)),
        ],
        compiler_params=pltpu.CompilerParams(vmem_limit_bytes=VMEM),
        cost_estimate=pl.CostEstimate(
            flops=2 * tokens * width * blocks * depth + followed_by,
            bytes_accessed=2**22,
            transcendentals=0,
        ),
    )(table, *sources, *parts, *extra)


def near_moves(table, sources, rows):
    near, away, rest = sources
    return [
        (near, rows.at[pl.ds(table[0] * SPLIT, SPLIT)]),
        (away, rows.at[pl.ds((1 - table[0]) * SPLIT, SPLIT)]),
        (rest.at[pl.ds(0, 2)], rows.at[pl.ds(2 * SPLIT, 2)]),
    ]


def last_moves(table, sources, rows):
    return [(sources[0].at[pl.ds(2, 2)], rows)]


def own_moves(table, sources, rows):
    return [
        (sources[0].at[:, pl.ds(pl.multiple_of(table[k], 128), rows.shape[2])], rows.at[k])
        for k in range(rows.shape[0])
    ]


def squares_kernel(where_ref, out_rows, *refs):
    blocks = out_rows.shape[0]
    in_rows, refs = refs[:blocks], refs[blocks:]
    totals, (outer, inner, semaphore) = refs[:2], refs[2:]
    copies = [pltpu.make_async_copy(out_rows, outer, semaphore.at[blocks])]
    for k in range(blocks):
        copies.append(
            pltpu.make_async_copy(in_rows[k], inner.at[where_ref[k]], semaphore.at[k])
        )
    for copy in copies:
        copy.start()
    for copy in copies:
        copy.wait()

    @pl.loop(0, inner.shape[2] // TILE)
    def _(n):
        columns = pl.ds(pl.multiple_of(n * TILE, TILE), TILE)
        for part, total_ref in enumerate(totals):
            half = where_ref[blocks + part]
            total = None
            for k in range(blocks):
                for example in range(EXAMPLES):
                    tokens = pl.ds(example * TOK, TOK)
                    rotated = dot(outer[k, half, :, tokens], inner[k, tokens, columns])
                    squared = rotated * rotated
                    total = squared if total is None else total + squared
            total_ref[:, columns] = total


TILE = 256


def sums_of_squares(where, out_rows, in_rows):
    rows, tokens = out_rows.shape[2:]
    width, blocks = in_rows[0].shape[1], len(in_rows)
    return pl.pallas_call(
        squares_kernel,
        out_shape=[jax.ShapeDtypeStruct((rows, width), jnp.float32)] * 2,
        in_specs=[space(pltpu.SMEM)] + [space(pl.ANY)] * (1 + blocks),
        out_specs=[space(pltpu.VMEM)] * 2,
        scratch_shapes=[
            pltpu.VMEM(out_rows.shape, jnp.bfloat16),
            pltpu.VMEM((blocks, tokens, width), jnp.bfloat16),
            pltpu.SemaphoreType.DMA((blocks + 1,)),
        ],
        compiler_params=pltpu.CompilerParams(vmem_limit_bytes=TAIL_VMEM),
        cost_estimate=pl.CostEstimate(
            flops=4 * rows * width * blocks * tokens,
            bytes_accessed=out_rows.size * 2 + rows * width * 8,
            transcendentals=0,
        ),
    )(where, out_rows, *in_rows)


def transposed(block):
    pairs = []
    for sx in range(NX):
        for sy in range(NY):
            for sc in range(NC):
                for t in range(NX * NY * NC):
                    source = ((sx * NY + sy) * NC + sc) * NH * NZ + t
                    target = (t // NC * NC + sc) * NH * NZ + t % NC * NZ + sx * NY + sy
                    pairs.append((source, target))
    return lax.ppermute(block, ("dp", "blk"), pairs)


def on_device(activations, out_grads, basis_in, basis_out):
    d, b = lax.axis_index("dp"), lax.axis_index("blk")
    core, y, x = d % NC, (d // NC) % NY, d // (NC * NY)
    parity = b % 2
    scale = 1.0 / float(EXAMPLES * NX * NY * NC)
    depth = basis_in.shape[0]
    spots = [((y + dy) % NY) * NC + (core + dc) % NC for dy, dc in BLOCKS]
    half = len(BLOCKS)

    table = jnp.stack(spots).astype(jnp.int32)
    give = (half * (1 - x) + table) * depth
    keep = ((half * x + table) * depth).astype(jnp.int32)
    near = lax.dynamic_slice_in_dim(give, parity * SPLIT, SPLIT)
    near = by_core(pieces(near.astype(jnp.int32), activations, depth), dx=1)
    left, right = shift(basis_in, dy=1), shift(basis_in, dy=3)
    own_other = shift(basis_in, dc=1)
    block = transposed(dot(out_grads, basis_out).astype(jnp.bfloat16).T)

    rest = pieces(give[2 * SPLIT :].astype(jnp.int32), activations, depth)
    near, rest, block = lax.optimization_barrier((near, rest, block))
    rest, away = by_core(rest, dx=1), by_core(near, dz=1)
    far = by_core(jnp.where(core == 0, left, right), dy=1)
    left_other, right_other = shift(left, dc=1), shift(right, dc=1)

    out_rows = lax.all_gather(
        jnp.stack([block, shift(block, dx=NX)]),
        "blk",
        axis=0,
        axis_index_groups=[[h * NZ + z for z in range(NZ)] for h in range(NH)],
    )
    flip = (b // NZ + core) % 2
    where = jnp.stack(
        [((x + dx) % NX) * NY + (y + dy) % NY for dx, dy in ORDER] + [flip, 1 - flip]
    ).astype(jnp.int32)

    panels = [basis_in, own_other, left, left_other, right, right_other, far, shift(far, dc=1)]
    panels = [[panel] for panel in panels]
    parity = parity.reshape(1).astype(jnp.int32)
    partial = product(near_moves, 3, parity, (near, away, rest), panels[:-2])
    partial = product(last_moves, 1, parity, (rest,), panels[-2:], partial, FOLLOWED)
    arrived = swap((partial * FACTOR).astype(jnp.float16))
    total = product(own_moves, len(BLOCKS), keep, (activations,), panels)
    proj_in = (total + arrived.astype(jnp.float32) * (1.0 / FACTOR)).astype(jnp.bfloat16)

    p_left, p_right, p_far = shift(proj_in, dy=1), shift(proj_in, dy=3), shift(proj_in, dy=2)
    p_across = swap(proj_in)
    px_left, px_right = shift(p_across, dy=1), shift(p_across, dy=3)
    px_far = swap(p_far)
    kept, given = sums_of_squares(
        where,
        out_rows,
        (proj_in, p_left, p_right, p_across, p_far, px_left, px_right, px_far),
    )
    return (kept + shift(given, dc=1)) * jnp.float32(scale)


def solution(mesh):
    return jax.shard_map(
        on_device,
        mesh=mesh,
        in_specs=(P("dp", None), P("dp", None), P("dp", "blk"), P(None, "blk")),
        out_specs=P("dp", "blk"),
        check_vma=False,
    )
```

```python
import jax
import jax.numpy as jnp
from jax import lax
from jax.experimental import pallas as pl
from jax.experimental.pallas import tpu as pltpu
from jax.sharding import PartitionSpec as P

TOK = 128
EXAMPLES = 2
NX, NY, NC = 2, 4, 2
NH, NZ = 2, 8
SPLIT = 2
FACTOR = 32.0
VMEM = 60 * 1024 * 1024
FOLLOWED = 6 * 10**9
TAIL_VMEM = 16 * 1024 * 1024
BLOCKS = ((0, 0), (0, 1), (3, 0), (1, 1), (1, 0), (3, 1), (2, 0), (2, 1))
ORDER = ((0, 0), (0, 3), (0, 1), (1, 0), (0, 2), (1, 3), (1, 1), (1, 2))


def index(x, y, z, c):
    return ((x % NX * NY + y) * NC + c) * NH * NZ + x // NX * NZ + z


def shift(value, dx=0, dy=0, dz=0, dc=0):
    size = NX * NH
    pairs = [
        (index(x, y, z, c), index((x + dx) % size, (y + dy) % NY, (z + dz) % NZ, (c + dc) % NC))
        for x in range(size)
        for y in range(NY)
        for z in range(NZ)
        for c in range(NC)
    ]
    return lax.ppermute(value, ("dp", "blk"), pairs)


def by_core(value, dx=0, dy=0, dz=0):
    size = NX * NH
    pairs = []
    for x in range(size):
        for y in range(NY):
            for z in range(NZ):
                for c, way in ((0, 1), (1, -1)):
                    target = ((x + way * dx) % size, (y + way * dy) % NY, (z + way * dz) % NZ, c)
                    pairs.append((index(x, y, z, c), index(*target)))
    return lax.ppermute(value, ("dp", "blk"), pairs)


def swap(value, dy=0):
    pairs = [
        (index(x, y, z, c), index(x ^ 1, (y + dy) % NY, z, c))
        for x in range(NX * NH)
        for y in range(NY)
        for z in range(NZ)
        for c in range(NC)
    ]
    return lax.ppermute(value, ("dp", "blk"), pairs)


def dot(a, b):
    return jnp.dot(a, b, preferred_element_type=jnp.float32)


def space(kind):
    return pl.BlockSpec(memory_space=kind)


def pieces_kernel(columns_ref, source, out, held, arrived, left):
    moves = []
    for k in range(held.shape[0]):
        column = pl.multiple_of(columns_ref[k], 128)
        get = source.at[:, pl.ds(column, held.shape[2])]
        moves.append(
            (
                pltpu.make_async_copy(get, held.at[k], arrived.at[k]),
                pltpu.make_async_copy(held.at[k], out.at[k], left.at[k]),
            )
        )
    for get, put in moves:
        get.start()
    for get, put in moves:
        get.wait()
        put.start()
    for get, put in moves:
        put.wait()


def pieces(columns, activations, depth):
    tokens, count = activations.shape[0], columns.shape[0]
    shape = (count, tokens, depth)
    return pl.pallas_call(
        pieces_kernel,
        out_shape=jax.ShapeDtypeStruct(shape, activations.dtype),
        in_specs=[space(pltpu.SMEM), space(pltpu.HBM)],
        out_specs=space(pltpu.HBM),
        scratch_shapes=[
            pltpu.VMEM(shape, activations.dtype),
            pltpu.SemaphoreType.DMA((count,)),
            pltpu.SemaphoreType.DMA((count,)),
        ],
        compiler_params=pltpu.CompilerParams(vmem_limit_bytes=VMEM),
        cost_estimate=pl.CostEstimate(flops=0, bytes_accessed=2**22, transcendentals=0),
    )(columns, activations)


def product_kernel(moves, layout, *refs):
    table, sources, refs = refs[0], refs[1 : 1 + layout[0]], refs[1 + layout[0] :]
    parts, refs = refs[: sum(layout[1])], refs[sum(layout[1]) :]
    before, (out, rows, panels, semaphore) = refs[:-4], refs[-4:]
    pairs = moves(table, sources, rows)
    for_rows = [pltpu.make_async_copy(*pair, semaphore.at[n]) for n, pair in enumerate(pairs)]
    for_panels, at = [], 0
    for k, count in enumerate(layout[1]):
        filled, copies = 0, []
        for part in parts[at : at + count]:
            target = panels.at[k, pl.ds(filled, part.shape[0])]
            number = len(pairs) + at + len(copies)
            copies.append(pltpu.make_async_copy(part, target, semaphore.at[number]))
            filled += part.shape[0]
        at += count
        for_panels.append(copies)
    for copy in for_rows + sum(for_panels, []):
        copy.start()
    for copy in for_rows:
        copy.wait()
    for k, copies in enumerate(for_panels):
        for copy in copies:
            copy.wait()
        term = dot(rows[k], panels[k])
        if k:
            out[...] += term
        else:
            out[...] = before[0][...] + term if before else term


def product(moves, count, table, sources, panels, before=None, followed_by=0, grant=VMEM):
    tokens, blocks = EXAMPLES * TOK, len(panels)
    depth, width = panels[0][0].shape[0] if len(panels[0]) == 1 else sum(
        part.shape[0] for part in panels[0]
    ), panels[0][0].shape[1]
    parts = sum(panels, [])
    layout = (len(sources), [len(panel) for panel in panels])
    extra = [] if before is None else [before]
    return pl.pallas_call(
        lambda *refs: product_kernel(moves, layout, *refs),
        out_shape=jax.ShapeDtypeStruct((tokens, width), jnp.float32),
        in_specs=[space(pltpu.SMEM)]
        + [space(pl.ANY)] * (len(sources) + len(parts))
        + [space(pltpu.VMEM)] * len(extra),
        out_specs=space(pltpu.VMEM),
        scratch_shapes=[
            pltpu.VMEM((blocks, tokens, depth), jnp.bfloat16),
            pltpu.VMEM((blocks, depth, width), jnp.bfloat16),
            pltpu.SemaphoreType.DMA((count + len(parts),)),
        ],
        compiler_params=pltpu.CompilerParams(vmem_limit_bytes=grant),
        cost_estimate=pl.CostEstimate(
            flops=2 * tokens * width * blocks * depth + followed_by,
            bytes_accessed=2**22,
            transcendentals=0,
        ),
    )(table, *sources, *parts, *extra)


def near_moves(table, sources, rows):
    near, away, rest = sources
    return [
        (near, rows.at[pl.ds(table[0] * SPLIT, SPLIT)]),
        (away, rows.at[pl.ds((1 - table[0]) * SPLIT, SPLIT)]),
        (rest.at[pl.ds(0, 2)], rows.at[pl.ds(2 * SPLIT, 2)]),
    ]


def last_moves(table, sources, rows):
    return [(sources[0].at[pl.ds(2, 2)], rows)]


def own_moves(table, sources, rows):
    return [
        (sources[0].at[:, pl.ds(pl.multiple_of(table[k], 128), rows.shape[2])], rows.at[k])
        for k in range(rows.shape[0])
    ]


def squares_kernel(where_ref, out_rows, *refs):
    blocks = out_rows.shape[0]
    in_rows, refs = refs[:blocks], refs[blocks:]
    totals, (outer, inner, semaphore) = refs[:2], refs[2:]
    copies = [pltpu.make_async_copy(out_rows, outer, semaphore.at[blocks])]
    for k in range(blocks):
        copies.append(
            pltpu.make_async_copy(in_rows[k], inner.at[where_ref[k]], semaphore.at[k])
        )
    for copy in copies:
        copy.start()
    for copy in copies:
        copy.wait()

    @pl.loop(0, inner.shape[2] // TILE)
    def _(n):
        columns = pl.ds(pl.multiple_of(n * TILE, TILE), TILE)
        for part, total_ref in enumerate(totals):
            half = where_ref[blocks + part]
            total = None
            for k in range(blocks):
                for example in range(EXAMPLES):
                    tokens = pl.ds(example * TOK, TOK)
                    rotated = dot(outer[k, half, :, tokens], inner[k, tokens, columns])
                    squared = rotated * rotated
                    total = squared if total is None else total + squared
            total_ref[:, columns] = total


TILE = 256


def sums_of_squares(where, out_rows, in_rows):
    rows, tokens = out_rows.shape[2:]
    width, blocks = in_rows[0].shape[1], len(in_rows)
    return pl.pallas_call(
        squares_kernel,
        out_shape=[jax.ShapeDtypeStruct((rows, width), jnp.float32)] * 2,
        in_specs=[space(pltpu.SMEM)] + [space(pl.ANY)] * (1 + blocks),
        out_specs=[space(pltpu.VMEM)] * 2,
        scratch_shapes=[
            pltpu.VMEM(out_rows.shape, jnp.bfloat16),
            pltpu.VMEM((blocks, tokens, width), jnp.bfloat16),
            pltpu.SemaphoreType.DMA((blocks + 1,)),
        ],
        compiler_params=pltpu.CompilerParams(vmem_limit_bytes=TAIL_VMEM),
        cost_estimate=pl.CostEstimate(
            flops=4 * rows * width * blocks * tokens,
            bytes_accessed=out_rows.size * 2 + rows * width * 8,
            transcendentals=0,
        ),
    )(where, out_rows, *in_rows)


def z_swap(value):
    pairs = []
    for d in range(NX * NY * NC):
        for b in range(NH * NZ):
            pairs.append((d * NH * NZ + b, d * NH * NZ + (b ^ 1)))
    return lax.ppermute(value, ("dp", "blk"), pairs)


def transposed(block):
    pairs = []
    for sx in range(NX):
        for sy in range(NY):
            for sc in range(NC):
                for t in range(NX * NY * NC):
                    source = ((sx * NY + sy) * NC + sc) * NH * NZ + t
                    target = (t // NC * NC + sc) * NH * NZ + t % NC * NZ + sx * NY + sy
                    pairs.append((source, target))
    return lax.ppermute(block, ("dp", "blk"), pairs)


def on_device(activations, out_grads, basis_in, basis_out):
    d, b = lax.axis_index("dp"), lax.axis_index("blk")
    core, y, x = d % NC, (d // NC) % NY, d // (NC * NY)
    parity = b % 2
    scale = 1.0 / float(EXAMPLES * NX * NY * NC)
    depth = basis_in.shape[0]
    mirror = 1 - 2 * core
    spots = [((y + mirror * dy) % NY) * NC + (core + dc) % NC for dy, dc in BLOCKS]
    half = len(BLOCKS)

    table = jnp.stack(spots).astype(jnp.int32)
    give = (half * (1 - x) + table) * depth
    keep = ((half * x + table) * depth).astype(jnp.int32)
    near = lax.dynamic_slice_in_dim(give, parity * SPLIT, SPLIT)
    near = by_core(pieces(near.astype(jnp.int32), activations, depth), dx=1)
    first, own_other = by_core(basis_in, dy=1), shift(basis_in, dc=1)
    rest = pieces(give[2 * SPLIT :].astype(jnp.int32), activations, depth)
    block = dot(out_grads, basis_out).astype(jnp.bfloat16).T
    block = transposed(jnp.stack([block, z_swap(block)]))

    first, near, rest, again, own_other = lax.optimization_barrier(
        (first, near, rest, basis_in, own_other)
    )
    second, far = by_core(again, dy=NY - 1), by_core(first, dy=1)
    rest, away = by_core(rest, dx=1), by_core(near, dz=1)

    out_rows = lax.all_gather(
        block,
        "blk",
        axis=0,
        axis_index_groups=[[h * NZ + z for z in range(NZ)] for h in range(NH)],
    )
    flip = (b // NZ + core) % 2
    where = jnp.stack(
        [((x + dx) % NX) * NY + (y + dy) % NY for dx, dy in ORDER] + [flip, 1 - flip]
    ).astype(jnp.int32)

    panels = []
    for panel in (first, second, far):
        panels += [panel, shift(panel, dc=1)]
    panels = [basis_in, own_other] + panels
    panels = [[panel] for panel in panels]
    parity = parity.reshape(1).astype(jnp.int32)
    partial = product(near_moves, 3, parity, (near, away, rest), panels[:-2])
    partial = product(last_moves, 1, parity, (rest,), panels[-2:], partial, FOLLOWED, TAIL_VMEM)
    arrived = swap((partial * FACTOR).astype(jnp.float16))
    total = product(own_moves, len(BLOCKS), keep, (activations,), panels)
    proj_in = (total + arrived.astype(jnp.float32) * (1.0 / FACTOR)).astype(jnp.bfloat16)

    p_left, p_right, p_far = shift(proj_in, dy=1), shift(proj_in, dy=3), shift(proj_in, dy=2)
    p_across = swap(proj_in)
    px_left, px_right = shift(p_across, dy=1), shift(p_across, dy=3)
    px_far = swap(p_far)
    kept, given = sums_of_squares(
        where,
        out_rows,
        (proj_in, p_left, p_right, p_across, p_far, px_left, px_right, px_far),
    )
    return (kept + shift(given, dc=1)) * jnp.float32(scale)


def solution(mesh):
    return jax.shard_map(
        on_device,
        mesh=mesh,
        in_specs=(P("dp", None), P("dp", None), P("dp", "blk"), P(None, "blk")),
        out_specs=P("dp", "blk"),
        check_vma=False,
    )
```

```python
import jax
import jax.numpy as jnp
from jax import lax
from jax.experimental import pallas as pl
from jax.experimental.pallas import tpu as pltpu
from jax.sharding import PartitionSpec as P

TOK = 128
EXAMPLES = 2
NX, NY, NC = 2, 4, 2
NH, NZ = 2, 8
SPLIT = 2
FACTOR = 32.0
VMEM = 60 * 1024 * 1024
FOLLOWED = 6 * 10**9
TAIL_VMEM = 16 * 1024 * 1024
BLOCKS = ((0, 0), (0, 1), (3, 0), (1, 1), (1, 0), (3, 1), (2, 0), (2, 1))
ORDER = ((0, 0), (0, 3), (0, 1), (1, 0), (0, 2), (1, 3), (1, 1), (1, 2))


def index(x, y, z, c):
    return ((x % NX * NY + y) * NC + c) * NH * NZ + x // NX * NZ + z


def shift(value, dx=0, dy=0, dz=0, dc=0):
    size = NX * NH
    pairs = [
        (index(x, y, z, c), index((x + dx) % size, (y + dy) % NY, (z + dz) % NZ, (c + dc) % NC))
        for x in range(size)
        for y in range(NY)
        for z in range(NZ)
        for c in range(NC)
    ]
    return lax.ppermute(value, ("dp", "blk"), pairs)


def by_core(value, dx=0, dy=0, dz=0):
    size = NX * NH
    pairs = []
    for x in range(size):
        for y in range(NY):
            for z in range(NZ):
                for c, way in ((0, 1), (1, -1)):
                    target = ((x + way * dx) % size, (y + way * dy) % NY, (z + way * dz) % NZ, c)
                    pairs.append((index(x, y, z, c), index(*target)))
    return lax.ppermute(value, ("dp", "blk"), pairs)


def swap(value, dy=0):
    pairs = [
        (index(x, y, z, c), index(x ^ 1, (y + dy) % NY, z, c))
        for x in range(NX * NH)
        for y in range(NY)
        for z in range(NZ)
        for c in range(NC)
    ]
    return lax.ppermute(value, ("dp", "blk"), pairs)


def dot(a, b):
    return jnp.dot(a, b, preferred_element_type=jnp.float32)


def space(kind):
    return pl.BlockSpec(memory_space=kind)


def pieces_kernel(columns_ref, source, out, held, arrived, left):
    moves = []
    for k in range(held.shape[0]):
        column = pl.multiple_of(columns_ref[k], 128)
        get = source.at[:, pl.ds(column, held.shape[2])]
        moves.append(
            (
                pltpu.make_async_copy(get, held.at[k], arrived.at[k]),
                pltpu.make_async_copy(held.at[k], out.at[k], left.at[k]),
            )
        )
    for get, put in moves:
        get.start()
    for get, put in moves:
        get.wait()
        put.start()
    for get, put in moves:
        put.wait()


def pieces(columns, activations, depth):
    tokens, count = activations.shape[0], columns.shape[0]
    shape = (count, tokens, depth)
    return pl.pallas_call(
        pieces_kernel,
        out_shape=jax.ShapeDtypeStruct(shape, activations.dtype),
        in_specs=[space(pltpu.SMEM), space(pltpu.HBM)],
        out_specs=space(pltpu.HBM),
        scratch_shapes=[
            pltpu.VMEM(shape, activations.dtype),
            pltpu.SemaphoreType.DMA((count,)),
            pltpu.SemaphoreType.DMA((count,)),
        ],
        compiler_params=pltpu.CompilerParams(vmem_limit_bytes=VMEM),
        cost_estimate=pl.CostEstimate(flops=0, bytes_accessed=2**22, transcendentals=0),
    )(columns, activations)


def product_kernel(moves, layout, *refs):
    table, sources, refs = refs[0], refs[1 : 1 + layout[0]], refs[1 + layout[0] :]
    parts, refs = refs[: sum(layout[1])], refs[sum(layout[1]) :]
    before, (out, rows, panels, semaphore) = refs[:-4], refs[-4:]
    pairs = moves(table, sources, rows)
    for_rows = [pltpu.make_async_copy(*pair, semaphore.at[n]) for n, pair in enumerate(pairs)]
    for_panels, at = [], 0
    for k, count in enumerate(layout[1]):
        filled, copies = 0, []
        for part in parts[at : at + count]:
            target = panels.at[k, pl.ds(filled, part.shape[0])]
            number = len(pairs) + at + len(copies)
            copies.append(pltpu.make_async_copy(part, target, semaphore.at[number]))
            filled += part.shape[0]
        at += count
        for_panels.append(copies)
    for copy in for_rows + sum(for_panels, []):
        copy.start()
    for copy in for_rows:
        copy.wait()
    for k, copies in enumerate(for_panels):
        for copy in copies:
            copy.wait()
        term = dot(rows[k], panels[k])
        if k:
            out[...] += term
        else:
            out[...] = before[0][...] + term if before else term


def product(moves, count, table, sources, panels, before=None, followed_by=0, grant=VMEM):
    tokens, blocks = EXAMPLES * TOK, len(panels)
    depth, width = panels[0][0].shape[0] if len(panels[0]) == 1 else sum(
        part.shape[0] for part in panels[0]
    ), panels[0][0].shape[1]
    parts = sum(panels, [])
    layout = (len(sources), [len(panel) for panel in panels])
    extra = [] if before is None else [before]
    return pl.pallas_call(
        lambda *refs: product_kernel(moves, layout, *refs),
        out_shape=jax.ShapeDtypeStruct((tokens, width), jnp.float32),
        in_specs=[space(pltpu.SMEM)]
        + [space(pl.ANY)] * (len(sources) + len(parts))
        + [space(pltpu.VMEM)] * len(extra),
        out_specs=space(pltpu.VMEM),
        scratch_shapes=[
            pltpu.VMEM((blocks, tokens, depth), jnp.bfloat16),
            pltpu.VMEM((blocks, depth, width), jnp.bfloat16),
            pltpu.SemaphoreType.DMA((count + len(parts),)),
        ],
        compiler_params=pltpu.CompilerParams(vmem_limit_bytes=grant),
        cost_estimate=pl.CostEstimate(
            flops=2 * tokens * width * blocks * depth + followed_by,
            bytes_accessed=2**22,
            transcendentals=0,
        ),
    )(table, *sources, *parts, *extra)


def near_moves(table, sources, rows):
    near, away = sources
    return [
        (near, rows.at[pl.ds(table[0] * SPLIT, SPLIT)]),
        (away, rows.at[pl.ds((1 - table[0]) * SPLIT, SPLIT)]),
    ]


def rest_moves(table, sources, rows):
    return [(source, rows.at[pl.ds(n * SPLIT, SPLIT)]) for n, source in enumerate(sources)]


def own_moves(table, sources, rows):
    return [
        (sources[0].at[:, pl.ds(pl.multiple_of(table[k], 128), rows.shape[2])], rows.at[k])
        for k in range(rows.shape[0])
    ]


def squares_kernel(blocks, where_ref, *refs):
    sources, refs = refs[: 2 * blocks], refs[2 * blocks :]
    totals, (outer, inner, semaphore) = refs[:2], refs[2:]
    copies = []
    for k in range(blocks):
        for n, target in ((k, outer), (blocks + k, inner)):
            copies.append(
                pltpu.make_async_copy(sources[n], target.at[where_ref[n]], semaphore.at[n])
            )
    for copy in copies:
        copy.start()
    for copy in copies:
        copy.wait()

    @pl.loop(0, inner.shape[2] // TILE)
    def _(n):
        columns = pl.ds(pl.multiple_of(n * TILE, TILE), TILE)
        for part, total_ref in enumerate(totals):
            half = where_ref[2 * blocks + part]
            total = None
            for k in range(blocks):
                for example in range(EXAMPLES):
                    tokens = pl.ds(example * TOK, TOK)
                    rotated = dot(outer[k, half, :, tokens], inner[k, tokens, columns])
                    squared = rotated * rotated
                    total = squared if total is None else total + squared
            total_ref[:, columns] = total


TILE = 256


def sums_of_squares(where, out_rows, in_rows):
    rows, tokens = out_rows[0].shape[1:]
    width, blocks = in_rows[0].shape[1], len(in_rows)
    return pl.pallas_call(
        lambda *refs: squares_kernel(blocks, *refs),
        out_shape=[jax.ShapeDtypeStruct((rows, width), jnp.float32)] * 2,
        in_specs=[space(pltpu.SMEM)] + [space(pl.ANY)] * (2 * blocks),
        out_specs=[space(pltpu.VMEM)] * 2,
        scratch_shapes=[
            pltpu.VMEM((blocks, *out_rows[0].shape), jnp.bfloat16),
            pltpu.VMEM((blocks, tokens, width), jnp.bfloat16),
            pltpu.SemaphoreType.DMA((2 * blocks,)),
        ],
        compiler_params=pltpu.CompilerParams(vmem_limit_bytes=TAIL_VMEM),
        cost_estimate=pl.CostEstimate(
            flops=4 * rows * width * blocks * tokens,
            bytes_accessed=2**22,
            transcendentals=0,
        ),
    )(where, *out_rows, *in_rows)


def z_swap(value):
    pairs = []
    for d in range(NX * NY * NC):
        for b in range(NH * NZ):
            pairs.append((d * NH * NZ + b, d * NH * NZ + (b ^ 1)))
    return lax.ppermute(value, ("dp", "blk"), pairs)


def transposed(block):
    pairs = []
    for sx in range(NX):
        for sy in range(NY):
            for sc in range(NC):
                for t in range(NX * NY * NC):
                    source = ((sx * NY + sy) * NC + sc) * NH * NZ + t
                    target = (t // NC * NC + sc) * NH * NZ + t % NC * NZ + sx * NY + sy
                    pairs.append((source, target))
    return lax.ppermute(block, ("dp", "blk"), pairs)


def on_device(activations, out_grads, basis_in, basis_out):
    d, b = lax.axis_index("dp"), lax.axis_index("blk")
    core, y, x = d % NC, (d // NC) % NY, d // (NC * NY)
    parity = b % 2
    scale = 1.0 / float(EXAMPLES * NX * NY * NC)
    depth = basis_in.shape[0]
    mirror = 1 - 2 * core
    spots = [((y + mirror * dy) % NY) * NC + (core + dc) % NC for dy, dc in BLOCKS]
    half = len(BLOCKS)

    table = jnp.stack(spots).astype(jnp.int32)
    give = (half * (1 - x) + table) * depth
    keep = ((half * x + table) * depth).astype(jnp.int32)
    first, own_other = by_core(basis_in, dy=1), shift(basis_in, dc=1)
    block = dot(out_grads, basis_out).astype(jnp.bfloat16).T
    block, source = lax.optimization_barrier((block, activations))
    near = lax.dynamic_slice_in_dim(give, parity * SPLIT, SPLIT)
    near = by_core(pieces(near.astype(jnp.int32), source, depth), dx=1)
    block, source = lax.optimization_barrier((jnp.stack([block, z_swap(block)]), source))
    later = give[2 * SPLIT :].astype(jnp.int32)
    rest_a = pieces(later[:SPLIT], source, depth)
    rest_b = pieces(later[SPLIT:], source, depth)

    first, near, rest_a, again, block, own_other = lax.optimization_barrier(
        (first, near, rest_a, basis_in, block, own_other)
    )
    second, rest_a, away = by_core(again, dy=NY - 1), by_core(rest_a, dx=1), by_core(near, dz=1)
    block, first_other = transposed(block), shift(first, dc=1)
    second, rest_a, away, block, onward, rest_b = lax.optimization_barrier(
        (second, rest_a, away, block, first, rest_b)
    )
    far, rest_b, second_other = by_core(onward, dy=1), by_core(rest_b, dx=1), shift(second, dc=1)

    up1, down1 = shift(block, dz=1), shift(block, dz=NZ - 1)
    far, up1, down1 = lax.optimization_barrier((far, up1, down1))
    up2, down2 = shift(up1, dz=1), shift(down1, dz=NZ - 1)
    h, z = b // NZ, b % NZ
    flip = (h + core) % 2
    where = jnp.stack(
        [(z - step) % NZ for step in range(NZ)]
        + [((x + dx) % NX) * NY + (y + dy) % NY for dx, dy in ORDER]
        + [flip, 1 - flip]
    ).astype(jnp.int32)

    panels = [basis_in, own_other, first, first_other]
    panels += [second, second_other, far, shift(far, dc=1)]
    panels = [[panel] for panel in panels]
    parity = parity.reshape(1).astype(jnp.int32)
    partial = product(near_moves, 2, parity, (near, away), panels[: 2 * SPLIT])
    partial = product(
        rest_moves, 2, parity, (rest_a, rest_b), panels[2 * SPLIT :], partial, FOLLOWED, TAIL_VMEM
    )
    arrived = swap((partial * FACTOR).astype(jnp.float16))
    arrived, up2, down2 = lax.optimization_barrier((arrived, up2, down2))
    up3, down3 = shift(up2, dz=1), shift(down2, dz=NZ - 1)
    total = product(own_moves, len(BLOCKS), keep, (activations,), panels)
    proj_in = (total + arrived.astype(jnp.float32) * (1.0 / FACTOR)).astype(jnp.bfloat16)

    p_left, p_right, p_far = shift(proj_in, dy=1), shift(proj_in, dy=3), shift(proj_in, dy=2)
    p_across = swap(proj_in)
    p_across, p_far, p_left, p_right, up3, down3 = lax.optimization_barrier(
        (p_across, p_far, p_left, p_right, up3, down3)
    )
    px_left, px_right = shift(p_across, dy=1), shift(p_across, dy=3)
    px_far = swap(p_far)
    opposite = by_core(jnp.where(core == 0, up3, down3), dz=1)
    out_rows = (block, up1, up2, up3, opposite, down3, down2, down1)
    kept, given = sums_of_squares(
        where,
        out_rows,
        (proj_in, p_left, p_right, p_across, p_far, px_left, px_right, px_far),
    )
    return (kept + shift(given, dc=1)) * jnp.float32(scale)


def solution(mesh):
    return jax.shard_map(
        on_device,
        mesh=mesh,
        in_specs=(P("dp", None), P("dp", None), P("dp", "blk"), P(None, "blk")),
        out_specs=P("dp", "blk"),
        check_vma=False,
    )
```

```python
import jax
import jax.numpy as jnp
from jax import lax
from jax.experimental import pallas as pl
from jax.experimental.pallas import tpu as pltpu
from jax.sharding import PartitionSpec as P

TOK = 128
EXAMPLES = 2
NX, NY, NC = 2, 4, 2
NH, NZ = 2, 8
SPLIT = 2
FACTOR = 32.0
VMEM = 60 * 1024 * 1024
FOLLOWED = 6 * 10**9
TAIL_VMEM = 16 * 1024 * 1024
BLOCKS = ((0, 0), (0, 1), (3, 0), (1, 1), (1, 0), (3, 1), (2, 0), (2, 1))
ORDER = ((0, 0), (0, 3), (0, 1), (1, 0), (0, 2), (1, 3), (1, 1), (1, 2))


def index(x, y, z, c):
    return ((x % NX * NY + y) * NC + c) * NH * NZ + x // NX * NZ + z


def shift(value, dx=0, dy=0, dz=0, dc=0):
    size = NX * NH
    pairs = [
        (index(x, y, z, c), index((x + dx) % size, (y + dy) % NY, (z + dz) % NZ, (c + dc) % NC))
        for x in range(size)
        for y in range(NY)
        for z in range(NZ)
        for c in range(NC)
    ]
    return lax.ppermute(value, ("dp", "blk"), pairs)


def by_core(value, dx=0, dy=0, dz=0):
    size = NX * NH
    pairs = []
    for x in range(size):
        for y in range(NY):
            for z in range(NZ):
                for c, way in ((0, 1), (1, -1)):
                    target = ((x + way * dx) % size, (y + way * dy) % NY, (z + way * dz) % NZ, c)
                    pairs.append((index(x, y, z, c), index(*target)))
    return lax.ppermute(value, ("dp", "blk"), pairs)


def swap(value, dy=0):
    pairs = [
        (index(x, y, z, c), index(x ^ 1, (y + dy) % NY, z, c))
        for x in range(NX * NH)
        for y in range(NY)
        for z in range(NZ)
        for c in range(NC)
    ]
    return lax.ppermute(value, ("dp", "blk"), pairs)


def dot(a, b):
    return jnp.dot(a, b, preferred_element_type=jnp.float32)


def space(kind):
    return pl.BlockSpec(memory_space=kind)


def pieces_kernel(columns_ref, source, out, held, arrived, left):
    moves = []
    for k in range(held.shape[0]):
        column = pl.multiple_of(columns_ref[k], 128)
        get = source.at[:, pl.ds(column, held.shape[2])]
        moves.append(
            (
                pltpu.make_async_copy(get, held.at[k], arrived.at[k]),
                pltpu.make_async_copy(held.at[k], out.at[k], left.at[k]),
            )
        )
    for get, put in moves:
        get.start()
    for get, put in moves:
        get.wait()
        put.start()
    for get, put in moves:
        put.wait()


def pieces(columns, activations, depth):
    tokens, count = activations.shape[0], columns.shape[0]
    shape = (count, tokens, depth)
    return pl.pallas_call(
        pieces_kernel,
        out_shape=jax.ShapeDtypeStruct(shape, activations.dtype),
        in_specs=[space(pltpu.SMEM), space(pltpu.HBM)],
        out_specs=space(pltpu.HBM),
        scratch_shapes=[
            pltpu.VMEM(shape, activations.dtype),
            pltpu.SemaphoreType.DMA((count,)),
            pltpu.SemaphoreType.DMA((count,)),
        ],
        compiler_params=pltpu.CompilerParams(vmem_limit_bytes=VMEM),
        cost_estimate=pl.CostEstimate(flops=0, bytes_accessed=2**22, transcendentals=0),
    )(columns, activations)


def product_kernel(moves, layout, *refs):
    table, sources, refs = refs[0], refs[1 : 1 + layout[0]], refs[1 + layout[0] :]
    parts, refs = refs[: sum(layout[1])], refs[sum(layout[1]) :]
    before, (out, rows, panels, semaphore) = refs[:-4], refs[-4:]
    pairs = moves(table, sources, rows)
    for_rows = [pltpu.make_async_copy(*pair, semaphore.at[n]) for n, pair in enumerate(pairs)]
    for_panels, at = [], 0
    for k, count in enumerate(layout[1]):
        filled, copies = 0, []
        for part in parts[at : at + count]:
            target = panels.at[k, pl.ds(filled, part.shape[0])]
            number = len(pairs) + at + len(copies)
            copies.append(pltpu.make_async_copy(part, target, semaphore.at[number]))
            filled += part.shape[0]
        at += count
        for_panels.append(copies)
    for copy in for_rows + sum(for_panels, []):
        copy.start()
    for copy in for_rows:
        copy.wait()
    for k, copies in enumerate(for_panels):
        for copy in copies:
            copy.wait()
        term = dot(rows[k], panels[k])
        if k:
            out[...] += term
        else:
            out[...] = before[0][...] + term if before else term


def product(moves, count, table, sources, panels, before=None, followed_by=0, grant=VMEM):
    tokens, blocks = EXAMPLES * TOK, len(panels)
    depth, width = panels[0][0].shape[0] if len(panels[0]) == 1 else sum(
        part.shape[0] for part in panels[0]
    ), panels[0][0].shape[1]
    parts = sum(panels, [])
    layout = (len(sources), [len(panel) for panel in panels])
    extra = [] if before is None else [before]
    return pl.pallas_call(
        lambda *refs: product_kernel(moves, layout, *refs),
        out_shape=jax.ShapeDtypeStruct((tokens, width), jnp.float32),
        in_specs=[space(pltpu.SMEM)]
        + [space(pl.ANY)] * (len(sources) + len(parts))
        + [space(pltpu.VMEM)] * len(extra),
        out_specs=space(pltpu.VMEM),
        scratch_shapes=[
            pltpu.VMEM((blocks, tokens, depth), jnp.bfloat16),
            pltpu.VMEM((blocks, depth, width), jnp.bfloat16),
            pltpu.SemaphoreType.DMA((count + len(parts),)),
        ],
        compiler_params=pltpu.CompilerParams(vmem_limit_bytes=grant),
        cost_estimate=pl.CostEstimate(
            flops=2 * tokens * width * blocks * depth + followed_by,
            bytes_accessed=2**22,
            transcendentals=0,
        ),
    )(table, *sources, *parts, *extra)


def near_moves(table, sources, rows):
    near, away = sources
    return [
        (near, rows.at[pl.ds(table[0] * SPLIT, SPLIT)]),
        (away, rows.at[pl.ds((1 - table[0]) * SPLIT, SPLIT)]),
    ]


def rest_moves(table, sources, rows):
    return [(sources[0], rows)]


def own_moves(table, sources, rows):
    return [
        (sources[0].at[:, pl.ds(pl.multiple_of(table[k], 128), rows.shape[2])], rows.at[k])
        for k in range(rows.shape[0])
    ]


def squares_kernel(blocks, where_ref, *refs):
    sources, refs = refs[: 2 * blocks], refs[2 * blocks :]
    totals, (outer, inner, semaphore) = refs[:2], refs[2:]
    copies = []
    for k in range(blocks):
        for n, target in ((k, outer), (blocks + k, inner)):
            copies.append(
                pltpu.make_async_copy(sources[n], target.at[where_ref[n]], semaphore.at[n])
            )
    for copy in copies:
        copy.start()
    for copy in copies:
        copy.wait()

    @pl.loop(0, inner.shape[2] // TILE)
    def _(n):
        columns = pl.ds(pl.multiple_of(n * TILE, TILE), TILE)
        for part, total_ref in enumerate(totals):
            half = where_ref[2 * blocks + part]
            total = None
            for k in range(blocks):
                for example in range(EXAMPLES):
                    tokens = pl.ds(example * TOK, TOK)
                    rotated = dot(outer[k, half, :, tokens], inner[k, tokens, columns])
                    squared = rotated * rotated
                    total = squared if total is None else total + squared
            total_ref[:, columns] = total


TILE = 256


def sums_of_squares(where, out_rows, in_rows):
    rows, tokens = out_rows[0].shape[1:]
    width, blocks = in_rows[0].shape[1], len(in_rows)
    return pl.pallas_call(
        lambda *refs: squares_kernel(blocks, *refs),
        out_shape=[jax.ShapeDtypeStruct((rows, width), jnp.float32)] * 2,
        in_specs=[space(pltpu.SMEM)] + [space(pl.ANY)] * (2 * blocks),
        out_specs=[space(pltpu.VMEM)] * 2,
        scratch_shapes=[
            pltpu.VMEM((blocks, *out_rows[0].shape), jnp.bfloat16),
            pltpu.VMEM((blocks, tokens, width), jnp.bfloat16),
            pltpu.SemaphoreType.DMA((2 * blocks,)),
        ],
        compiler_params=pltpu.CompilerParams(vmem_limit_bytes=TAIL_VMEM),
        cost_estimate=pl.CostEstimate(
            flops=4 * rows * width * blocks * tokens,
            bytes_accessed=2**22,
            transcendentals=0,
        ),
    )(where, *out_rows, *in_rows)


def transposed(block):
    pairs = []
    for sx in range(NX):
        for sy in range(NY):
            for sc in range(NC):
                for t in range(NX * NY * NC):
                    source = ((sx * NY + sy) * NC + sc) * NH * NZ + t
                    target = (t // NC * NC + sc) * NH * NZ + t % NC * NZ + sx * NY + sy
                    pairs.append((source, target))
    return lax.ppermute(block, ("dp", "blk"), pairs)


def on_device(activations, out_grads, basis_in, basis_out):
    d, b = lax.axis_index("dp"), lax.axis_index("blk")
    core, y, x = d % NC, (d // NC) % NY, d // (NC * NY)
    parity = b % 2
    scale = 1.0 / float(EXAMPLES * NX * NY * NC)
    depth = basis_in.shape[0]
    mirror = 1 - 2 * core
    spots = [((y + mirror * dy) % NY) * NC + (core + dc) % NC for dy, dc in BLOCKS]
    half = len(BLOCKS)

    table = jnp.stack(spots).astype(jnp.int32)
    give = (half * (1 - x) + table) * depth
    keep = ((half * x + table) * depth).astype(jnp.int32)
    first, own_other = by_core(basis_in, dy=1), shift(basis_in, dc=1)
    near = lax.dynamic_slice_in_dim(give, parity * SPLIT, SPLIT)
    near = pieces(near.astype(jnp.int32), activations, depth)
    block = transposed(dot(out_grads, basis_out).astype(jnp.bfloat16).T)
    near, block = lax.optimization_barrier((near, block))
    near, other = by_core(near, dx=1), shift(block, dx=NX)
    rest = pieces(give[2 * SPLIT :].astype(jnp.int32), activations, depth)
    first, again = lax.optimization_barrier((first, basis_in))
    second, first_other = by_core(again, dy=NY - 1), shift(first, dc=1)

    block = jnp.stack([block, other])
    up1, down1 = shift(block, dz=1), shift(block, dz=NZ - 1)
    near, second, up1, down1, rest, first = lax.optimization_barrier(
        (near, second, up1, down1, rest, first)
    )
    far, rest, away = by_core(first, dy=1), by_core(rest, dx=1), by_core(near, dz=1)
    up2, down2 = shift(up1, dz=1), shift(down1, dz=NZ - 1)
    second_other = shift(second, dc=1)
    far, away, up2, down2 = lax.optimization_barrier((far, away, up2, down2))
    up3, down3 = shift(up2, dz=1), shift(down2, dz=NZ - 1)
    h, z = b // NZ, b % NZ
    flip = (h + core) % 2
    where = jnp.stack(
        [(z - step) % NZ for step in range(NZ)]
        + [((x + dx) % NX) * NY + (y + dy) % NY for dx, dy in ORDER]
        + [flip, 1 - flip]
    ).astype(jnp.int32)

    panels = [basis_in, own_other, first, first_other]
    panels += [second, second_other, far, shift(far, dc=1)]
    panels = [[panel] for panel in panels]
    parity = parity.reshape(1).astype(jnp.int32)
    partial = product(near_moves, 2, parity, (near, away), panels[: 2 * SPLIT])
    rest, up3, down3 = lax.optimization_barrier((rest, up3, down3))
    opposite = by_core(jnp.where(core == 0, up3, down3), dz=1)
    out_rows = (block, up1, up2, up3, opposite, down3, down2, down1)
    partial = product(
        rest_moves, 1, parity, (rest,), panels[2 * SPLIT :], partial, FOLLOWED, TAIL_VMEM
    )
    arrived = swap((partial * FACTOR).astype(jnp.float16))
    total = product(own_moves, len(BLOCKS), keep, (activations,), panels)
    proj_in = (total + arrived.astype(jnp.float32) * (1.0 / FACTOR)).astype(jnp.bfloat16)

    p_left, p_right, p_far = shift(proj_in, dy=1), shift(proj_in, dy=3), shift(proj_in, dy=2)
    p_across = swap(proj_in)
    px_left, px_right = shift(p_across, dy=1), shift(p_across, dy=3)
    px_far = swap(p_far)
    kept, given = sums_of_squares(
        where,
        out_rows,
        (proj_in, p_left, p_right, p_across, p_far, px_left, px_right, px_far),
    )
    return (kept + shift(given, dc=1)) * jnp.float32(scale)


def solution(mesh):
    return jax.shard_map(
        on_device,
        mesh=mesh,
        in_specs=(P("dp", None), P("dp", None), P("dp", "blk"), P(None, "blk")),
        out_specs=P("dp", "blk"),
        check_vma=False,
    )
```

```python
import jax
import jax.numpy as jnp
from jax import lax
from jax.experimental import pallas as pl
from jax.experimental.pallas import tpu as pltpu
from jax.sharding import PartitionSpec as P

TOK = 128
EXAMPLES = 2
NX, NY, NC = 2, 4, 2
NH, NZ = 2, 8
SPLIT = 2
FACTOR = 32.0
VMEM = 60 * 1024 * 1024
FOLLOWED = 6 * 10**9
TAIL_VMEM = 16 * 1024 * 1024
BLOCKS = ((0, 0), (0, 1), (3, 0), (1, 1), (1, 0), (3, 1), (2, 0), (2, 1))
ORDER = ((0, 0), (0, 3), (0, 1), (1, 0), (0, 2), (1, 3), (1, 1), (1, 2))


def index(x, y, z, c):
    return ((x % NX * NY + y) * NC + c) * NH * NZ + x // NX * NZ + z


def shift(value, dx=0, dy=0, dz=0, dc=0):
    size = NX * NH
    pairs = [
        (index(x, y, z, c), index((x + dx) % size, (y + dy) % NY, (z + dz) % NZ, (c + dc) % NC))
        for x in range(size)
        for y in range(NY)
        for z in range(NZ)
        for c in range(NC)
    ]
    return lax.ppermute(value, ("dp", "blk"), pairs)


def by_core(value, dx=0, dy=0, dz=0):
    size = NX * NH
    pairs = []
    for x in range(size):
        for y in range(NY):
            for z in range(NZ):
                for c, way in ((0, 1), (1, -1)):
                    target = ((x + way * dx) % size, (y + way * dy) % NY, (z + way * dz) % NZ, c)
                    pairs.append((index(x, y, z, c), index(*target)))
    return lax.ppermute(value, ("dp", "blk"), pairs)


def swap(value, dy=0):
    pairs = [
        (index(x, y, z, c), index(x ^ 1, (y + dy) % NY, z, c))
        for x in range(NX * NH)
        for y in range(NY)
        for z in range(NZ)
        for c in range(NC)
    ]
    return lax.ppermute(value, ("dp", "blk"), pairs)


def dot(a, b):
    return jnp.dot(a, b, preferred_element_type=jnp.float32)


def space(kind):
    return pl.BlockSpec(memory_space=kind)


def pieces_kernel(columns_ref, source, out, held, arrived, left):
    moves = []
    for k in range(held.shape[0]):
        column = pl.multiple_of(columns_ref[k], 128)
        get = source.at[:, pl.ds(column, held.shape[2])]
        moves.append(
            (
                pltpu.make_async_copy(get, held.at[k], arrived.at[k]),
                pltpu.make_async_copy(held.at[k], out.at[k], left.at[k]),
            )
        )
    for get, put in moves:
        get.start()
    for get, put in moves:
        get.wait()
        put.start()
    for get, put in moves:
        put.wait()


def pieces(columns, activations, depth):
    tokens, count = activations.shape[0], columns.shape[0]
    shape = (count, tokens, depth)
    return pl.pallas_call(
        pieces_kernel,
        out_shape=jax.ShapeDtypeStruct(shape, activations.dtype),
        in_specs=[space(pltpu.SMEM), space(pltpu.HBM)],
        out_specs=space(pltpu.HBM),
        scratch_shapes=[
            pltpu.VMEM(shape, activations.dtype),
            pltpu.SemaphoreType.DMA((count,)),
            pltpu.SemaphoreType.DMA((count,)),
        ],
        compiler_params=pltpu.CompilerParams(vmem_limit_bytes=VMEM),
        cost_estimate=pl.CostEstimate(flops=0, bytes_accessed=2**22, transcendentals=0),
    )(columns, activations)


def product_kernel(moves, layout, *refs):
    table, sources, refs = refs[0], refs[1 : 1 + layout[0]], refs[1 + layout[0] :]
    parts, refs = refs[: sum(layout[1])], refs[sum(layout[1]) :]
    before, (out, rows, panels, semaphore) = refs[:-4], refs[-4:]
    pairs = moves(table, sources, rows)
    for_rows = [pltpu.make_async_copy(*pair, semaphore.at[n]) for n, pair in enumerate(pairs)]
    for_panels, at = [], 0
    for k, count in enumerate(layout[1]):
        filled, copies = 0, []
        for part in parts[at : at + count]:
            target = panels.at[k, pl.ds(filled, part.shape[0])]
            number = len(pairs) + at + len(copies)
            copies.append(pltpu.make_async_copy(part, target, semaphore.at[number]))
            filled += part.shape[0]
        at += count
        for_panels.append(copies)
    for copy in for_rows + sum(for_panels, []):
        copy.start()
    for copy in for_rows:
        copy.wait()
    for k, copies in enumerate(for_panels):
        for copy in copies:
            copy.wait()
        term = dot(rows[k], panels[k])
        if k:
            out[...] += term
        else:
            out[...] = before[0][...] + term if before else term


def product(moves, count, table, sources, panels, before=None, followed_by=0, grant=VMEM):
    tokens, blocks = EXAMPLES * TOK, len(panels)
    depth, width = panels[0][0].shape[0] if len(panels[0]) == 1 else sum(
        part.shape[0] for part in panels[0]
    ), panels[0][0].shape[1]
    parts = sum(panels, [])
    layout = (len(sources), [len(panel) for panel in panels])
    extra = [] if before is None else [before]
    return pl.pallas_call(
        lambda *refs: product_kernel(moves, layout, *refs),
        out_shape=jax.ShapeDtypeStruct((tokens, width), jnp.float32),
        in_specs=[space(pltpu.SMEM)]
        + [space(pl.ANY)] * (len(sources) + len(parts))
        + [space(pltpu.VMEM)] * len(extra),
        out_specs=space(pltpu.VMEM),
        scratch_shapes=[
            pltpu.VMEM((blocks, tokens, depth), jnp.bfloat16),
            pltpu.VMEM((blocks, depth, width), jnp.bfloat16),
            pltpu.SemaphoreType.DMA((count + len(parts),)),
        ],
        compiler_params=pltpu.CompilerParams(vmem_limit_bytes=grant),
        cost_estimate=pl.CostEstimate(
            flops=2 * tokens * width * blocks * depth + followed_by,
            bytes_accessed=2**22,
            transcendentals=0,
        ),
    )(table, *sources, *parts, *extra)


def near_moves(table, sources, rows):
    near, away = sources
    return [
        (near, rows.at[pl.ds(table[0] * SPLIT, SPLIT)]),
        (away, rows.at[pl.ds((1 - table[0]) * SPLIT, SPLIT)]),
    ]


def rest_moves(table, sources, rows):
    return [(sources[0], rows)]


def own_moves(table, sources, rows):
    return [
        (sources[0].at[:, pl.ds(pl.multiple_of(table[k], 128), rows.shape[2])], rows.at[k])
        for k in range(rows.shape[0])
    ]


def squares_kernel(where_ref, out_rows, *refs):
    blocks = out_rows.shape[0]
    in_rows, refs = refs[:blocks], refs[blocks:]
    totals, (outer, inner, semaphore) = refs[:2], refs[2:]
    copies = [pltpu.make_async_copy(out_rows, outer, semaphore.at[blocks])]
    for k in range(blocks):
        copies.append(
            pltpu.make_async_copy(in_rows[k], inner.at[k], semaphore.at[k])
        )
    for copy in copies:
        copy.start()
    for copy in copies:
        copy.wait()

    @pl.loop(0, inner.shape[2] // TILE)
    def _(n):
        columns = pl.ds(pl.multiple_of(n * TILE, TILE), TILE)
        for part, total_ref in enumerate(totals):
            total = None
            for k in range(blocks):
                at, half = where_ref[k] + where_ref[2 * blocks + part], where_ref[blocks + k]
                for example in range(EXAMPLES):
                    tokens = pl.ds(example * TOK, TOK)
                    rotated = dot(outer[at, half, :, tokens], inner[k, tokens, columns])
                    squared = rotated * rotated
                    total = squared if total is None else total + squared
            total_ref[:, columns] = total


TILE = 256


def sums_of_squares(where, out_rows, in_rows):
    rows, tokens = out_rows.shape[2:]
    width, blocks = in_rows[0].shape[1], len(in_rows)
    return pl.pallas_call(
        squares_kernel,
        out_shape=[jax.ShapeDtypeStruct((rows, width), jnp.float32)] * 2,
        in_specs=[space(pltpu.SMEM)] + [space(pl.ANY)] * (1 + blocks),
        out_specs=[space(pltpu.VMEM)] * 2,
        scratch_shapes=[
            pltpu.VMEM(out_rows.shape, jnp.bfloat16),
            pltpu.VMEM((blocks, tokens, width), jnp.bfloat16),
            pltpu.SemaphoreType.DMA((blocks + 1,)),
        ],
        compiler_params=pltpu.CompilerParams(vmem_limit_bytes=TAIL_VMEM),
        cost_estimate=pl.CostEstimate(
            flops=4 * rows * width * blocks * tokens,
            bytes_accessed=out_rows.size * 2 + rows * width * 8,
            transcendentals=0,
        ),
    )(where, out_rows, *in_rows)


def transposed(block):
    pairs = []
    for sx in range(NX):
        for sy in range(NY):
            for sc in range(NC):
                for t in range(NX * NY * NC):
                    source = ((sx * NY + sy) * NC + sc) * NH * NZ + t
                    target = (t // NC * NC + sc) * NH * NZ + sx * NZ + sy * NC + t % NC
                    pairs.append((source, target))
    return lax.ppermute(block, ("dp", "blk"), pairs)


def on_device(activations, out_grads, basis_in, basis_out):
    d, b = lax.axis_index("dp"), lax.axis_index("blk")
    core, y, x = d % NC, (d // NC) % NY, d // (NC * NY)
    parity = b % 2
    scale = 1.0 / float(EXAMPLES * NX * NY * NC)
    depth = basis_in.shape[0]
    mirror = 1 - 2 * core
    spots = [((y + mirror * dy) % NY) * NC + (core + dc) % NC for dy, dc in BLOCKS]
    half = len(BLOCKS)

    table = jnp.stack(spots).astype(jnp.int32)
    give = (half * (1 - x) + table) * depth
    keep = ((half * x + table) * depth).astype(jnp.int32)
    first, own_other = by_core(basis_in, dy=1), shift(basis_in, dc=1)
    block = dot(out_grads, basis_out).astype(jnp.bfloat16).T
    block, source = lax.optimization_barrier((block, activations))
    near = lax.dynamic_slice_in_dim(give, parity * SPLIT, SPLIT)
    near = by_core(pieces(near.astype(jnp.int32), source, depth), dx=1)
    rest = pieces(give[2 * SPLIT :].astype(jnp.int32), source, depth)
    first, near, rest, again, own_other, block = lax.optimization_barrier(
        (first, near, rest, basis_in, own_other, transposed(block))
    )
    second, far = by_core(again, dy=NY - 1), by_core(first, dy=1)
    rest, away = by_core(rest, dx=1), by_core(near, dz=1)
    first_other = shift(first, dc=1)

    other = lax.optimization_barrier((shift(block, dx=NX), second, away))[0]
    out_rows = lax.all_gather(
        jnp.stack([block, other]),
        "blk",
        axis=0,
        axis_index_groups=[[h * NZ + z for z in range(NZ)] for h in range(NH)],
    )
    where = jnp.stack(
        [(y + dy) % NY * NC for dx, dy in ORDER]
        + [(x + dx + b // NZ) % 2 for dx, dy in ORDER]
        + [core, 1 - core]
    ).astype(jnp.int32)

    panels = [basis_in, own_other, first, first_other]
    for panel in (second, far):
        panels += [panel, shift(panel, dc=1)]
    panels = [[panel] for panel in panels]
    parity = parity.reshape(1).astype(jnp.int32)
    partial = product(near_moves, 2, parity, (near, away), panels[: 2 * SPLIT])
    partial = product(
        rest_moves, 1, parity, (rest,), panels[2 * SPLIT :], partial, FOLLOWED, TAIL_VMEM
    )
    arrived = swap((partial * FACTOR).astype(jnp.float16))
    total = product(own_moves, len(BLOCKS), keep, (activations,), panels)
    proj_in = (total + arrived.astype(jnp.float32) * (1.0 / FACTOR)).astype(jnp.bfloat16)

    p_left, p_right, p_far = shift(proj_in, dy=1), shift(proj_in, dy=3), shift(proj_in, dy=2)
    p_across = swap(proj_in)
    px_left, px_right = shift(p_across, dy=1), shift(p_across, dy=3)
    px_far = swap(p_far)
    kept, given = sums_of_squares(
        where,
        out_rows,
        (proj_in, p_left, p_right, p_across, p_far, px_left, px_right, px_far),
    )
    return (kept + shift(given, dc=1)) * jnp.float32(scale)


def solution(mesh):
    return jax.shard_map(
        on_device,
        mesh=mesh,
        in_specs=(P("dp", None), P("dp", None), P("dp", "blk"), P(None, "blk")),
        out_specs=P("dp", "blk"),
        check_vma=False,
    )
```

```python
import jax
import jax.numpy as jnp
from jax import lax
from jax.experimental import pallas as pl
from jax.experimental.pallas import tpu as pltpu
from jax.sharding import PartitionSpec as P

TOK = 128
EXAMPLES = 2
NX, NY, NC = 2, 4, 2
NH, NZ = 2, 8
SPLIT = 2
FACTOR = 32.0
VMEM = 60 * 1024 * 1024
FOLLOWED = 6 * 10**9
TAIL_VMEM = 16 * 1024 * 1024
BLOCKS = ((0, 0), (0, 1), (3, 0), (1, 1), (1, 0), (3, 1), (2, 0), (2, 1))
ORDER = ((0, 0), (0, 3), (0, 1), (1, 0), (0, 2), (1, 3), (1, 1), (1, 2))


def index(x, y, z, c):
    return ((x % NX * NY + y) * NC + c) * NH * NZ + x // NX * NZ + z


def shift(value, dx=0, dy=0, dz=0, dc=0):
    size = NX * NH
    pairs = [
        (index(x, y, z, c), index((x + dx) % size, (y + dy) % NY, (z + dz) % NZ, (c + dc) % NC))
        for x in range(size)
        for y in range(NY)
        for z in range(NZ)
        for c in range(NC)
    ]
    return lax.ppermute(value, ("dp", "blk"), pairs)


def by_core(value, dx=0, dy=0, dz=0):
    size = NX * NH
    pairs = []
    for x in range(size):
        for y in range(NY):
            for z in range(NZ):
                for c, way in ((0, 1), (1, -1)):
                    target = ((x + way * dx) % size, (y + way * dy) % NY, (z + way * dz) % NZ, c)
                    pairs.append((index(x, y, z, c), index(*target)))
    return lax.ppermute(value, ("dp", "blk"), pairs)


def swap(value, dy=0):
    pairs = [
        (index(x, y, z, c), index(x ^ 1, (y + dy) % NY, z, c))
        for x in range(NX * NH)
        for y in range(NY)
        for z in range(NZ)
        for c in range(NC)
    ]
    return lax.ppermute(value, ("dp", "blk"), pairs)


def dot(a, b):
    return jnp.dot(a, b, preferred_element_type=jnp.float32)


def space(kind):
    return pl.BlockSpec(memory_space=kind)


def pieces_kernel(columns_ref, source, out, held, arrived, left):
    moves = []
    for k in range(held.shape[0]):
        column = pl.multiple_of(columns_ref[k], 128)
        get = source.at[:, pl.ds(column, held.shape[2])]
        moves.append(
            (
                pltpu.make_async_copy(get, held.at[k], arrived.at[k]),
                pltpu.make_async_copy(held.at[k], out.at[k], left.at[k]),
            )
        )
    for get, put in moves:
        get.start()
    for get, put in moves:
        get.wait()
        put.start()
    for get, put in moves:
        put.wait()


def pieces(columns, activations, depth):
    tokens, count = activations.shape[0], columns.shape[0]
    shape = (count, tokens, depth)
    return pl.pallas_call(
        pieces_kernel,
        out_shape=jax.ShapeDtypeStruct(shape, activations.dtype),
        in_specs=[space(pltpu.SMEM), space(pltpu.HBM)],
        out_specs=space(pltpu.HBM),
        scratch_shapes=[
            pltpu.VMEM(shape, activations.dtype),
            pltpu.SemaphoreType.DMA((count,)),
            pltpu.SemaphoreType.DMA((count,)),
        ],
        compiler_params=pltpu.CompilerParams(vmem_limit_bytes=VMEM),
        cost_estimate=pl.CostEstimate(flops=0, bytes_accessed=2**22, transcendentals=0),
    )(columns, activations)


def product_kernel(moves, layout, *refs):
    table, sources, refs = refs[0], refs[1 : 1 + layout[0]], refs[1 + layout[0] :]
    parts, refs = refs[: sum(layout[1])], refs[sum(layout[1]) :]
    before, (out, rows, panels, semaphore) = refs[:-4], refs[-4:]
    pairs = moves(table, sources, rows)
    for_rows = [pltpu.make_async_copy(*pair, semaphore.at[n]) for n, pair in enumerate(pairs)]
    for_panels, at = [], 0
    for k, count in enumerate(layout[1]):
        filled, copies = 0, []
        for part in parts[at : at + count]:
            target = panels.at[k, pl.ds(filled, part.shape[0])]
            number = len(pairs) + at + len(copies)
            copies.append(pltpu.make_async_copy(part, target, semaphore.at[number]))
            filled += part.shape[0]
        at += count
        for_panels.append(copies)
    for copy in for_rows + sum(for_panels, []):
        copy.start()
    for copy in for_rows:
        copy.wait()
    for k, copies in enumerate(for_panels):
        for copy in copies:
            copy.wait()
        term = dot(rows[k], panels[k])
        if k:
            out[...] += term
        else:
            out[...] = before[0][...] + term if before else term


def product(moves, count, table, sources, panels, before=None, followed_by=0, grant=VMEM):
    tokens, blocks = EXAMPLES * TOK, len(panels)
    depth, width = panels[0][0].shape[0] if len(panels[0]) == 1 else sum(
        part.shape[0] for part in panels[0]
    ), panels[0][0].shape[1]
    parts = sum(panels, [])
    layout = (len(sources), [len(panel) for panel in panels])
    extra = [] if before is None else [before]
    return pl.pallas_call(
        lambda *refs: product_kernel(moves, layout, *refs),
        out_shape=jax.ShapeDtypeStruct((tokens, width), jnp.float32),
        in_specs=[space(pltpu.SMEM)]
        + [space(pl.ANY)] * (len(sources) + len(parts))
        + [space(pltpu.VMEM)] * len(extra),
        out_specs=space(pltpu.VMEM),
        scratch_shapes=[
            pltpu.VMEM((blocks, tokens, depth), jnp.bfloat16),
            pltpu.VMEM((blocks, depth, width), jnp.bfloat16),
            pltpu.SemaphoreType.DMA((count + len(parts),)),
        ],
        compiler_params=pltpu.CompilerParams(vmem_limit_bytes=grant),
        cost_estimate=pl.CostEstimate(
            flops=2 * tokens * width * blocks * depth + followed_by,
            bytes_accessed=2**22,
            transcendentals=0,
        ),
    )(table, *sources, *parts, *extra)


def near_moves(table, sources, rows):
    near, away = sources
    return [
        (near, rows.at[pl.ds(table[0] * SPLIT, SPLIT)]),
        (away, rows.at[pl.ds((1 - table[0]) * SPLIT, SPLIT)]),
    ]


def rest_moves(table, sources, rows):
    return [(sources[0], rows)]


def own_moves(table, sources, rows):
    return [
        (sources[0].at[:, pl.ds(pl.multiple_of(table[k], 128), rows.shape[2])], rows.at[k])
        for k in range(rows.shape[0])
    ]


def squares_kernel(where_ref, out_rows, *refs):
    blocks = out_rows.shape[0]
    in_rows, refs = refs[:blocks], refs[blocks:]
    totals, (outer, inner, semaphore) = refs[:2], refs[2:]
    copies = [pltpu.make_async_copy(out_rows, outer, semaphore.at[blocks])]
    for k in range(blocks):
        copies.append(
            pltpu.make_async_copy(in_rows[k], inner.at[k], semaphore.at[k])
        )
    for copy in copies:
        copy.start()
    for copy in copies:
        copy.wait()

    @pl.loop(0, inner.shape[2] // TILE)
    def _(n):
        columns = pl.ds(pl.multiple_of(n * TILE, TILE), TILE)
        for part, total_ref in enumerate(totals):
            total = None
            for k in range(blocks):
                at, half = where_ref[k] + where_ref[2 * blocks + part], where_ref[blocks + k]
                for example in range(EXAMPLES):
                    tokens = pl.ds(example * TOK, TOK)
                    rotated = dot(outer[at, half, :, tokens], inner[k, tokens, columns])
                    squared = rotated * rotated
                    total = squared if total is None else total + squared
            total_ref[:, columns] = total


TILE = 256


def sums_of_squares(where, out_rows, in_rows):
    rows, tokens = out_rows.shape[2:]
    width, blocks = in_rows[0].shape[1], len(in_rows)
    return pl.pallas_call(
        squares_kernel,
        out_shape=[jax.ShapeDtypeStruct((rows, width), jnp.float32)] * 2,
        in_specs=[space(pltpu.SMEM)] + [space(pl.ANY)] * (1 + blocks),
        out_specs=[space(pltpu.VMEM)] * 2,
        scratch_shapes=[
            pltpu.VMEM(out_rows.shape, jnp.bfloat16),
            pltpu.VMEM((blocks, tokens, width), jnp.bfloat16),
            pltpu.SemaphoreType.DMA((blocks + 1,)),
        ],
        compiler_params=pltpu.CompilerParams(vmem_limit_bytes=TAIL_VMEM),
        cost_estimate=pl.CostEstimate(
            flops=4 * rows * width * blocks * tokens,
            bytes_accessed=out_rows.size * 2 + rows * width * 8,
            transcendentals=0,
        ),
    )(where, out_rows, *in_rows)


def transposed(block):
    pairs = []
    for sx in range(NX):
        for sy in range(NY):
            for sc in range(NC):
                for t in range(NX * NY * NC):
                    source = ((sx * NY + sy) * NC + sc) * NH * NZ + t
                    target = (t // NC * NC + sc) * NH * NZ + sx * NZ + sy * NC + t % NC
                    pairs.append((source, target))
    return lax.ppermute(block, ("dp", "blk"), pairs)


def on_device(activations, out_grads, basis_in, basis_out):
    d, b = lax.axis_index("dp"), lax.axis_index("blk")
    core, y, x = d % NC, (d // NC) % NY, d // (NC * NY)
    parity = b % 2
    scale = 1.0 / float(EXAMPLES * NX * NY * NC)
    depth = basis_in.shape[0]
    mirror = 1 - 2 * core
    spots = [((y + mirror * dy) % NY) * NC + (core + dc) % NC for dy, dc in BLOCKS]
    half = len(BLOCKS)

    table = jnp.stack(spots).astype(jnp.int32)
    give = (half * (1 - x) + table) * depth
    keep = ((half * x + table) * depth).astype(jnp.int32)
    first, own_other = by_core(basis_in, dy=1), shift(basis_in, dc=1)
    near = lax.dynamic_slice_in_dim(give, parity * SPLIT, SPLIT)
    near = pieces(near.astype(jnp.int32), activations, depth)
    rest = pieces(give[2 * SPLIT :].astype(jnp.int32), activations, depth)
    block = transposed(dot(out_grads, basis_out).astype(jnp.bfloat16).T)
    near, rest, block = lax.optimization_barrier((near, rest, block))
    near = by_core(near, dx=1)
    first, again = lax.optimization_barrier((first, basis_in))
    second, far = by_core(again, dy=NY - 1), by_core(first, dy=1)
    first_other = shift(first, dc=1)
    near, rest = lax.optimization_barrier((near, rest))
    rest, away = by_core(rest, dx=1), by_core(near, dz=1)

    other = shift(block, dx=NX)
    out_rows = lax.all_gather(
        jnp.stack([block, other]),
        "blk",
        axis=0,
        axis_index_groups=[[h * NZ + z for z in range(NZ)] for h in range(NH)],
    )
    where = jnp.stack(
        [(y + dy) % NY * NC for dx, dy in ORDER]
        + [(x + dx + b // NZ) % 2 for dx, dy in ORDER]
        + [core, 1 - core]
    ).astype(jnp.int32)

    panels = [basis_in, own_other, first, first_other]
    for panel in (second, far):
        panels += [panel, shift(panel, dc=1)]
    panels = [[panel] for panel in panels]
    parity = parity.reshape(1).astype(jnp.int32)
    partial = product(near_moves, 2, parity, (near, away), panels[: 2 * SPLIT])
    partial = product(
        rest_moves, 1, parity, (rest,), panels[2 * SPLIT :], partial, FOLLOWED, TAIL_VMEM
    )
    arrived = swap((partial * FACTOR).astype(jnp.float16))
    total = product(own_moves, len(BLOCKS), keep, (activations,), panels)
    proj_in = (total + arrived.astype(jnp.float32) * (1.0 / FACTOR)).astype(jnp.bfloat16)

    p_left, p_right, p_far = shift(proj_in, dy=1), shift(proj_in, dy=3), shift(proj_in, dy=2)
    p_across = swap(proj_in)
    px_left, px_right = shift(p_across, dy=1), shift(p_across, dy=3)
    px_far = swap(p_far)
    kept, given = sums_of_squares(
        where,
        out_rows,
        (proj_in, p_left, p_right, p_across, p_far, px_left, px_right, px_far),
    )
    return (kept + shift(given, dc=1)) * jnp.float32(scale)


def solution(mesh):
    return jax.shard_map(
        on_device,
        mesh=mesh,
        in_specs=(P("dp", None), P("dp", None), P("dp", "blk"), P(None, "blk")),
        out_specs=P("dp", "blk"),
        check_vma=False,
    )
```

```python
import jax
import jax.numpy as jnp
from jax import lax
from jax.experimental import pallas as pl
from jax.experimental.pallas import tpu as pltpu
from jax.sharding import PartitionSpec as P

TOK = 128
EXAMPLES = 2
NX, NY, NC = 2, 4, 2
NH, NZ = 2, 8
SPLIT = 2
FACTOR = 32.0
VMEM = 60 * 1024 * 1024
FOLLOWED = 6 * 10**9
TAIL_VMEM = 16 * 1024 * 1024
OWN_VMEM = 48 * 1024 * 1024
BLOCKS = ((0, 0), (0, 1), (3, 0), (1, 1), (1, 0), (3, 1), (2, 0), (2, 1))
ORDER = ((0, 0), (0, 3), (0, 1), (1, 0), (0, 2), (1, 3), (1, 1), (1, 2))


def index(x, y, z, c):
    return ((x % NX * NY + y) * NC + c) * NH * NZ + x // NX * NZ + z


def shift(value, dx=0, dy=0, dz=0, dc=0):
    size = NX * NH
    pairs = [
        (index(x, y, z, c), index((x + dx) % size, (y + dy) % NY, (z + dz) % NZ, (c + dc) % NC))
        for x in range(size)
        for y in range(NY)
        for z in range(NZ)
        for c in range(NC)
    ]
    return lax.ppermute(value, ("dp", "blk"), pairs)


def by_core(value, dx=0, dy=0, dz=0):
    size = NX * NH
    pairs = []
    for x in range(size):
        for y in range(NY):
            for z in range(NZ):
                for c, way in ((0, 1), (1, -1)):
                    target = ((x + way * dx) % size, (y + way * dy) % NY, (z + way * dz) % NZ, c)
                    pairs.append((index(x, y, z, c), index(*target)))
    return lax.ppermute(value, ("dp", "blk"), pairs)


def swap(value, dy=0):
    pairs = [
        (index(x, y, z, c), index(x ^ 1, (y + dy) % NY, z, c))
        for x in range(NX * NH)
        for y in range(NY)
        for z in range(NZ)
        for c in range(NC)
    ]
    return lax.ppermute(value, ("dp", "blk"), pairs)


def dot(a, b):
    return jnp.dot(a, b, preferred_element_type=jnp.float32)


def space(kind):
    return pl.BlockSpec(memory_space=kind)


def pieces_kernel(columns_ref, source, out, held, arrived, left):
    moves = []
    for k in range(held.shape[0]):
        column = pl.multiple_of(columns_ref[k], 128)
        get = source.at[:, pl.ds(column, held.shape[2])]
        moves.append(
            (
                pltpu.make_async_copy(get, held.at[k], arrived.at[k]),
                pltpu.make_async_copy(held.at[k], out.at[k], left.at[k]),
            )
        )
    for get, put in moves:
        get.start()
    for get, put in moves:
        get.wait()
        put.start()
    for get, put in moves:
        put.wait()


def pieces(columns, activations, depth):
    tokens, count = activations.shape[0], columns.shape[0]
    shape = (count, tokens, depth)
    return pl.pallas_call(
        pieces_kernel,
        out_shape=jax.ShapeDtypeStruct(shape, activations.dtype),
        in_specs=[space(pltpu.SMEM), space(pltpu.HBM)],
        out_specs=space(pltpu.HBM),
        scratch_shapes=[
            pltpu.VMEM(shape, activations.dtype),
            pltpu.SemaphoreType.DMA((count,)),
            pltpu.SemaphoreType.DMA((count,)),
        ],
        compiler_params=pltpu.CompilerParams(vmem_limit_bytes=VMEM),
        cost_estimate=pl.CostEstimate(flops=0, bytes_accessed=2**22, transcendentals=0),
    )(columns, activations)


def product_kernel(moves, layout, *refs):
    table, sources, refs = refs[0], refs[1 : 1 + layout[0]], refs[1 + layout[0] :]
    parts, refs = refs[: sum(layout[1])], refs[sum(layout[1]) :]
    before, (out, rows, panels, semaphore) = refs[:-4], refs[-4:]
    pairs = moves(table, sources, rows)
    for_rows = [pltpu.make_async_copy(*pair, semaphore.at[n]) for n, pair in enumerate(pairs)]
    for_panels, at = [], 0
    for k, count in enumerate(layout[1]):
        filled, copies = 0, []
        for part in parts[at : at + count]:
            target = panels.at[k, pl.ds(filled, part.shape[0])]
            number = len(pairs) + at + len(copies)
            copies.append(pltpu.make_async_copy(part, target, semaphore.at[number]))
            filled += part.shape[0]
        at += count
        for_panels.append(copies)
    if before:
        carry = pltpu.make_async_copy(before[0], out, semaphore.at[len(pairs) + len(parts)])
        carry.start()
    for copy in for_rows + sum(for_panels, []):
        copy.start()
    for copy in for_rows:
        copy.wait()
    for k, copies in enumerate(for_panels):
        for copy in copies:
            copy.wait()
        term = dot(rows[k], panels[k])
        if before and not k:
            carry.wait()
        if k or before:
            out[...] += term
        else:
            out[...] = term


def product(moves, count, table, sources, panels, before=None, followed_by=0, grant=VMEM):
    tokens, blocks = EXAMPLES * TOK, len(panels)
    depth, width = panels[0][0].shape[0] if len(panels[0]) == 1 else sum(
        part.shape[0] for part in panels[0]
    ), panels[0][0].shape[1]
    parts = sum(panels, [])
    layout = (len(sources), [len(panel) for panel in panels])
    extra = [] if before is None else [before]
    return pl.pallas_call(
        lambda *refs: product_kernel(moves, layout, *refs),
        out_shape=jax.ShapeDtypeStruct((tokens, width), jnp.float32),
        in_specs=[space(pltpu.SMEM)]
        + [space(pl.ANY)] * (len(sources) + len(parts) + len(extra)),
        out_specs=space(pltpu.VMEM),
        scratch_shapes=[
            pltpu.VMEM((blocks, tokens, depth), jnp.bfloat16),
            pltpu.VMEM((blocks, depth, width), jnp.bfloat16),
            pltpu.SemaphoreType.DMA((count + len(parts) + len(extra),)),
        ],
        compiler_params=pltpu.CompilerParams(vmem_limit_bytes=grant),
        cost_estimate=pl.CostEstimate(
            flops=2 * tokens * width * blocks * depth + followed_by,
            bytes_accessed=2**22,
            transcendentals=0,
        ),
    )(table, *sources, *parts, *extra)


def near_moves(table, sources, rows):
    near, away = sources
    return [
        (near, rows.at[pl.ds(table[0] * SPLIT, SPLIT)]),
        (away, rows.at[pl.ds((1 - table[0]) * SPLIT, SPLIT)]),
    ]


def rest_moves(table, sources, rows):
    return [(sources[0], rows)]


def own_moves(table, sources, rows):
    return [
        (sources[0].at[:, pl.ds(pl.multiple_of(table[k], 128), rows.shape[2])], rows.at[k])
        for k in range(rows.shape[0])
    ]


def squares_kernel(where_ref, out_rows, *refs):
    blocks = out_rows.shape[0]
    in_rows, refs = refs[:blocks], refs[blocks:]
    totals, (inner, semaphore) = refs[:2], refs[2:]
    copies = [
        pltpu.make_async_copy(in_rows[k], inner.at[k], semaphore.at[k]) for k in range(blocks)
    ]
    for copy in copies:
        copy.start()
    for copy in copies:
        copy.wait()

    @pl.loop(0, inner.shape[2] // TILE)
    def _(n):
        columns = pl.ds(pl.multiple_of(n * TILE, TILE), TILE)
        for part, total_ref in enumerate(totals):
            total = None
            for k in range(blocks):
                at, half = where_ref[k] + where_ref[2 * blocks + part], where_ref[blocks + k]
                for example in range(EXAMPLES):
                    tokens = pl.ds(example * TOK, TOK)
                    rotated = dot(out_rows[at, half, :, tokens], inner[k, tokens, columns])
                    squared = rotated * rotated
                    total = squared if total is None else total + squared
            total_ref[:, columns] = total


TILE = 256


def sums_of_squares(where, out_rows, in_rows):
    rows, tokens = out_rows.shape[2:]
    width, blocks = in_rows[0].shape[1], len(in_rows)
    return pl.pallas_call(
        squares_kernel,
        out_shape=[jax.ShapeDtypeStruct((rows, width), jnp.float32)] * 2,
        in_specs=[space(pltpu.SMEM), space(pltpu.VMEM)] + [space(pl.ANY)] * blocks,
        out_specs=[space(pltpu.VMEM)] * 2,
        scratch_shapes=[
            pltpu.VMEM((blocks, tokens, width), jnp.bfloat16),
            pltpu.SemaphoreType.DMA((blocks,)),
        ],
        compiler_params=pltpu.CompilerParams(vmem_limit_bytes=TAIL_VMEM),
        cost_estimate=pl.CostEstimate(
            flops=4 * rows * width * blocks * tokens,
            bytes_accessed=out_rows.size * 2 + rows * width * 8,
            transcendentals=0,
        ),
    )(where, out_rows, *in_rows)


def transposed(block):
    pairs = []
    for sx in range(NX):
        for sy in range(NY):
            for sc in range(NC):
                for t in range(NX * NY * NC):
                    source = ((sx * NY + sy) * NC + sc) * NH * NZ + t
                    target = (t // NC * NC + sc) * NH * NZ + sx * NZ + sy * NC + t % NC
                    pairs.append((source, target))
    return lax.ppermute(block, ("dp", "blk"), pairs)


def on_device(activations, out_grads, basis_in, basis_out):
    d, b = lax.axis_index("dp"), lax.axis_index("blk")
    core, y, x = d % NC, (d // NC) % NY, d // (NC * NY)
    parity = b % 2
    scale = 1.0 / float(EXAMPLES * NX * NY * NC)
    depth = basis_in.shape[0]
    mirror = 1 - 2 * core
    spots = [((y + mirror * dy) % NY) * NC + (core + dc) % NC for dy, dc in BLOCKS]
    half = len(BLOCKS)

    table = jnp.stack(spots).astype(jnp.int32)
    give = (half * (1 - x) + table) * depth
    keep = ((half * x + table) * depth).astype(jnp.int32)
    first, own_other = by_core(basis_in, dy=1), shift(basis_in, dc=1)
    near = lax.dynamic_slice_in_dim(give, parity * SPLIT, SPLIT)
    near = pieces(near.astype(jnp.int32), activations, depth)
    rest = pieces(give[2 * SPLIT :].astype(jnp.int32), activations, depth)
    block = transposed(dot(out_grads, basis_out).astype(jnp.bfloat16).T)
    near, block = lax.optimization_barrier((near, block))
    near = by_core(near, dx=1)
    first, again = lax.optimization_barrier((first, basis_in))
    second, far = by_core(again, dy=NY - 1), by_core(first, dy=1)
    first_other = shift(first, dc=1)
    near, rest = lax.optimization_barrier((near, rest))
    rest, away = by_core(rest, dx=1), by_core(near, dz=1)

    other = shift(block, dx=NX)
    out_rows = lax.all_gather(
        jnp.stack([block, other]),
        "blk",
        axis=0,
        axis_index_groups=[[h * NZ + z for z in range(NZ)] for h in range(NH)],
    )
    where = jnp.stack(
        [(y + dy) % NY * NC for dx, dy in ORDER]
        + [(x + dx + b // NZ) % 2 for dx, dy in ORDER]
        + [core, 1 - core]
    ).astype(jnp.int32)

    panels = [basis_in, own_other, first, first_other]
    for panel in (second, far):
        panels += [panel, shift(panel, dc=1)]
    panels = [[panel] for panel in panels]
    parity = parity.reshape(1).astype(jnp.int32)
    mine = product(own_moves, 2 * SPLIT, keep[: 2 * SPLIT], (activations,), panels[: 2 * SPLIT])
    mine, away = lax.optimization_barrier((mine, away))
    partial = product(
        near_moves, 2, parity, (near, away), panels[: 2 * SPLIT], None, 0, OWN_VMEM
    )
    partial = product(
        rest_moves, 1, parity, (rest,), panels[2 * SPLIT :], partial, FOLLOWED, TAIL_VMEM
    )
    arrived = swap((partial * FACTOR).astype(jnp.float16))
    total = product(
        own_moves, 2 * SPLIT, keep[2 * SPLIT :], (activations,), panels[2 * SPLIT :], mine, 0, OWN_VMEM
    )
    proj_in = (total + arrived.astype(jnp.float32) * (1.0 / FACTOR)).astype(jnp.bfloat16)

    p_left, p_right, p_far = shift(proj_in, dy=1), shift(proj_in, dy=3), shift(proj_in, dy=2)
    p_across = swap(proj_in)
    px_left, px_right = shift(p_across, dy=1), shift(p_across, dy=3)
    px_far = swap(p_far)
    kept, given = sums_of_squares(
        where,
        out_rows,
        (proj_in, p_left, p_right, p_across, p_far, px_left, px_right, px_far),
    )
    return (kept + shift(given, dc=1)) * jnp.float32(scale)


def solution(mesh):
    return jax.shard_map(
        on_device,
        mesh=mesh,
        in_specs=(P("dp", None), P("dp", None), P("dp", "blk"), P(None, "blk")),
        out_specs=P("dp", "blk"),
        check_vma=False,
    )
```

```python
import jax
import jax.numpy as jnp
from jax import lax
from jax.experimental import pallas as pl
from jax.experimental.pallas import tpu as pltpu
from jax.sharding import PartitionSpec as P

TOK = 128
EXAMPLES = 2
NX, NY, NC = 2, 4, 2
NH, NZ = 2, 8
SPLIT = 2
FACTOR = 32.0
VMEM = 60 * 1024 * 1024
FOLLOWED = 6 * 10**9
TAIL_VMEM = 16 * 1024 * 1024
OWN_VMEM = 48 * 1024 * 1024
BLOCKS = ((0, 0), (0, 1), (3, 0), (1, 1), (1, 0), (3, 1), (2, 0), (2, 1))
ORDER = ((0, 0), (0, 3), (0, 1), (1, 0), (0, 2), (1, 3), (1, 1), (1, 2))


def index(x, y, z, c):
    return ((x % NX * NY + y) * NC + c) * NH * NZ + x // NX * NZ + z


def shift(value, dx=0, dy=0, dz=0, dc=0):
    size = NX * NH
    pairs = [
        (index(x, y, z, c), index((x + dx) % size, (y + dy) % NY, (z + dz) % NZ, (c + dc) % NC))
        for x in range(size)
        for y in range(NY)
        for z in range(NZ)
        for c in range(NC)
    ]
    return lax.ppermute(value, ("dp", "blk"), pairs)


def by_core(value, dx=0, dy=0, dz=0):
    size = NX * NH
    pairs = []
    for x in range(size):
        for y in range(NY):
            for z in range(NZ):
                for c, way in ((0, 1), (1, -1)):
                    target = ((x + way * dx) % size, (y + way * dy) % NY, (z + way * dz) % NZ, c)
                    pairs.append((index(x, y, z, c), index(*target)))
    return lax.ppermute(value, ("dp", "blk"), pairs)


def swap(value, dy=0):
    pairs = [
        (index(x, y, z, c), index(x ^ 1, (y + dy) % NY, z, c))
        for x in range(NX * NH)
        for y in range(NY)
        for z in range(NZ)
        for c in range(NC)
    ]
    return lax.ppermute(value, ("dp", "blk"), pairs)


def dot(a, b):
    return jnp.dot(a, b, preferred_element_type=jnp.float32)


def space(kind):
    return pl.BlockSpec(memory_space=kind)


def pieces_kernel(columns_ref, source, out, held, arrived, left):
    moves = []
    for k in range(held.shape[0]):
        column = pl.multiple_of(columns_ref[k], 128)
        get = source.at[:, pl.ds(column, held.shape[2])]
        moves.append(
            (
                pltpu.make_async_copy(get, held.at[k], arrived.at[k]),
                pltpu.make_async_copy(held.at[k], out.at[k], left.at[k]),
            )
        )
    for get, put in moves:
        get.start()
    for get, put in moves:
        get.wait()
        put.start()
    for get, put in moves:
        put.wait()


def pieces(columns, activations, depth):
    tokens, count = activations.shape[0], columns.shape[0]
    shape = (count, tokens, depth)
    return pl.pallas_call(
        pieces_kernel,
        out_shape=jax.ShapeDtypeStruct(shape, activations.dtype),
        in_specs=[space(pltpu.SMEM), space(pltpu.HBM)],
        out_specs=space(pltpu.HBM),
        scratch_shapes=[
            pltpu.VMEM(shape, activations.dtype),
            pltpu.SemaphoreType.DMA((count,)),
            pltpu.SemaphoreType.DMA((count,)),
        ],
        compiler_params=pltpu.CompilerParams(vmem_limit_bytes=VMEM),
        cost_estimate=pl.CostEstimate(flops=0, bytes_accessed=2**22, transcendentals=0),
    )(columns, activations)


def product_kernel(moves, layout, *refs):
    table, sources, refs = refs[0], refs[1 : 1 + layout[0]], refs[1 + layout[0] :]
    parts, refs = refs[: sum(layout[1])], refs[sum(layout[1]) :]
    before, (out, rows, panels, semaphore) = refs[:-4], refs[-4:]
    pairs = moves(table, sources, rows)
    for_rows = [pltpu.make_async_copy(*pair, semaphore.at[n]) for n, pair in enumerate(pairs)]
    for_panels, at = [], 0
    for k, count in enumerate(layout[1]):
        filled, copies = 0, []
        for part in parts[at : at + count]:
            target = panels.at[k, pl.ds(filled, part.shape[0])]
            number = len(pairs) + at + len(copies)
            copies.append(pltpu.make_async_copy(part, target, semaphore.at[number]))
            filled += part.shape[0]
        at += count
        for_panels.append(copies)
    if before:
        carry = pltpu.make_async_copy(before[0], out, semaphore.at[len(pairs) + len(parts)])
        carry.start()
    for copy in for_rows + sum(for_panels, []):
        copy.start()
    for copy in for_rows:
        copy.wait()
    for k, copies in enumerate(for_panels):
        for copy in copies:
            copy.wait()
        term = dot(rows[k], panels[k])
        if before and not k:
            carry.wait()
        if k or before:
            out[...] += term
        else:
            out[...] = term


def product(moves, count, table, sources, panels, before=None, followed_by=0, grant=VMEM):
    tokens, blocks = EXAMPLES * TOK, len(panels)
    depth, width = panels[0][0].shape[0] if len(panels[0]) == 1 else sum(
        part.shape[0] for part in panels[0]
    ), panels[0][0].shape[1]
    parts = sum(panels, [])
    layout = (len(sources), [len(panel) for panel in panels])
    extra = [] if before is None else [before]
    return pl.pallas_call(
        lambda *refs: product_kernel(moves, layout, *refs),
        out_shape=jax.ShapeDtypeStruct((tokens, width), jnp.float32),
        in_specs=[space(pltpu.SMEM)]
        + [space(pl.ANY)] * (len(sources) + len(parts) + len(extra)),
        out_specs=space(pltpu.VMEM),
        scratch_shapes=[
            pltpu.VMEM((blocks, tokens, depth), jnp.bfloat16),
            pltpu.VMEM((blocks, depth, width), jnp.bfloat16),
            pltpu.SemaphoreType.DMA((count + len(parts) + len(extra),)),
        ],
        compiler_params=pltpu.CompilerParams(vmem_limit_bytes=grant),
        cost_estimate=pl.CostEstimate(
            flops=2 * tokens * width * blocks * depth + followed_by,
            bytes_accessed=2**22,
            transcendentals=0,
        ),
    )(table, *sources, *parts, *extra)


def near_moves(table, sources, rows):
    near, away = sources
    return [
        (near, rows.at[pl.ds(table[0] * SPLIT, SPLIT)]),
        (away, rows.at[pl.ds((1 - table[0]) * SPLIT, SPLIT)]),
    ]


def rest_moves(table, sources, rows):
    return [(sources[0], rows)]


def own_moves(table, sources, rows):
    return [
        (sources[0].at[:, pl.ds(pl.multiple_of(table[k], 128), rows.shape[2])], rows.at[k])
        for k in range(rows.shape[0])
    ]


def squares_kernel(where_ref, out_rows, *refs):
    blocks = out_rows.shape[0]
    in_rows, refs = refs[:blocks], refs[blocks:]
    totals, (inner, semaphore) = refs[:2], refs[2:]
    copies = [
        pltpu.make_async_copy(in_rows[k], inner.at[k], semaphore.at[k]) for k in range(blocks)
    ]
    for copy in copies:
        copy.start()
    for copy in copies:
        copy.wait()

    @pl.loop(0, inner.shape[2] // TILE)
    def _(n):
        columns = pl.ds(pl.multiple_of(n * TILE, TILE), TILE)
        for part, total_ref in enumerate(totals):
            total = None
            for k in range(blocks):
                at, half = where_ref[k] + where_ref[2 * blocks + part], where_ref[blocks + k]
                for example in range(EXAMPLES):
                    tokens = pl.ds(example * TOK, TOK)
                    rotated = dot(out_rows[at, half, :, tokens], inner[k, tokens, columns])
                    squared = rotated * rotated
                    total = squared if total is None else total + squared
            total_ref[:, columns] = total


TILE = 256


def sums_of_squares(where, out_rows, in_rows):
    rows, tokens = out_rows.shape[2:]
    width, blocks = in_rows[0].shape[1], len(in_rows)
    return pl.pallas_call(
        squares_kernel,
        out_shape=[jax.ShapeDtypeStruct((rows, width), jnp.float32)] * 2,
        in_specs=[space(pltpu.SMEM), space(pltpu.VMEM)] + [space(pl.ANY)] * blocks,
        out_specs=[space(pltpu.VMEM)] * 2,
        scratch_shapes=[
            pltpu.VMEM((blocks, tokens, width), jnp.bfloat16),
            pltpu.SemaphoreType.DMA((blocks,)),
        ],
        compiler_params=pltpu.CompilerParams(vmem_limit_bytes=TAIL_VMEM),
        cost_estimate=pl.CostEstimate(
            flops=4 * rows * width * blocks * tokens,
            bytes_accessed=out_rows.size * 2 + rows * width * 8,
            transcendentals=0,
        ),
    )(where, out_rows, *in_rows)


def transposed(block):
    pairs = []
    for sx in range(NX):
        for sy in range(NY):
            for sc in range(NC):
                for t in range(NX * NY * NC):
                    source = ((sx * NY + sy) * NC + sc) * NH * NZ + t
                    target = (t // NC * NC + sc) * NH * NZ + sx * NZ + sy * NC + t % NC
                    pairs.append((source, target))
    return lax.ppermute(block, ("dp", "blk"), pairs)


def on_device(activations, out_grads, basis_in, basis_out):
    d, b = lax.axis_index("dp"), lax.axis_index("blk")
    core, y, x = d % NC, (d // NC) % NY, d // (NC * NY)
    parity = b % 2
    scale = 1.0 / float(EXAMPLES * NX * NY * NC)
    depth = basis_in.shape[0]
    mirror = 1 - 2 * core
    spots = [((y + mirror * dy) % NY) * NC + (core + dc) % NC for dy, dc in BLOCKS]
    half = len(BLOCKS)

    table = jnp.stack(spots).astype(jnp.int32)
    give = (half * (1 - x) + table) * depth
    keep = ((half * x + table) * depth).astype(jnp.int32)
    first, own_other = by_core(basis_in, dy=1), shift(basis_in, dc=1)
    near = lax.dynamic_slice_in_dim(give, parity * SPLIT, SPLIT)
    near = pieces(near.astype(jnp.int32), activations, depth)
    rest = pieces(give[2 * SPLIT :].astype(jnp.int32), activations, depth)
    block = transposed(dot(out_grads, basis_out).astype(jnp.bfloat16).T)
    near, block = lax.optimization_barrier((near, block))
    near = by_core(near, dx=1)
    first, again = lax.optimization_barrier((first, basis_in))
    second, far = by_core(again, dy=NY - 1), by_core(first, dy=1)
    near, rest = lax.optimization_barrier((near, rest))
    rest, away = by_core(rest, dx=1), by_core(near, dz=1)

    other, first = lax.optimization_barrier((shift(block, dx=NX), first))
    first_other = shift(first, dc=1)
    out_rows = lax.all_gather(
        jnp.stack([block, other]),
        "blk",
        axis=0,
        axis_index_groups=[[h * NZ + z for z in range(NZ)] for h in range(NH)],
    )
    where = jnp.stack(
        [(y + dy) % NY * NC for dx, dy in ORDER]
        + [(x + dx + b // NZ) % 2 for dx, dy in ORDER]
        + [core, 1 - core]
    ).astype(jnp.int32)

    panels = [[panel] for panel in (basis_in, own_other, first, first_other)]
    mine = product(own_moves, 2 * SPLIT, keep[: 2 * SPLIT], (activations,), panels)
    mine, second = lax.optimization_barrier((mine, second))
    for panel in (second, far):
        panels += [[panel], [shift(panel, dc=1)]]
    parity = parity.reshape(1).astype(jnp.int32)
    partial = product(
        near_moves, 2, parity, (near, away), panels[: 2 * SPLIT], None, 0, OWN_VMEM
    )
    partial = product(
        rest_moves, 1, parity, (rest,), panels[2 * SPLIT :], partial, FOLLOWED, TAIL_VMEM
    )
    arrived = swap((partial * FACTOR).astype(jnp.float16))
    total = product(
        own_moves, 2 * SPLIT, keep[2 * SPLIT :], (activations,), panels[2 * SPLIT :], mine, 0, OWN_VMEM
    )
    proj_in = (total + arrived.astype(jnp.float32) * (1.0 / FACTOR)).astype(jnp.bfloat16)

    p_left, p_right, p_far = shift(proj_in, dy=1), shift(proj_in, dy=3), shift(proj_in, dy=2)
    p_across = swap(proj_in)
    px_left, px_right = shift(p_across, dy=1), shift(p_across, dy=3)
    px_far = swap(p_far)
    kept, given = sums_of_squares(
        where,
        out_rows,
        (proj_in, p_left, p_right, p_across, p_far, px_left, px_right, px_far),
    )
    return (kept + shift(given, dc=1)) * jnp.float32(scale)


def solution(mesh):
    return jax.shard_map(
        on_device,
        mesh=mesh,
        in_specs=(P("dp", None), P("dp", None), P("dp", "blk"), P(None, "blk")),
        out_specs=P("dp", "blk"),
        check_vma=False,
    )
```

```python
import jax
import jax.numpy as jnp
from jax import lax
from jax.experimental import pallas as pl
from jax.experimental.pallas import tpu as pltpu
from jax.sharding import PartitionSpec as P

TOK = 128
EXAMPLES = 2
NX, NY, NC = 2, 4, 2
NH, NZ = 2, 8
SPLIT = 2
FACTOR = 32.0
VMEM = 60 * 1024 * 1024
FOLLOWED = 10 * 10**9
TAIL_VMEM = 16 * 1024 * 1024
OWN_VMEM = 48 * 1024 * 1024
BLOCKS = ((0, 0), (0, 1), (3, 0), (1, 1), (1, 0), (3, 1), (2, 0), (2, 1))
ORDER = ((0, 0), (0, 3), (0, 1), (1, 0), (0, 2), (1, 3), (1, 1), (1, 2))


def index(x, y, z, c):
    return ((x % NX * NY + y) * NC + c) * NH * NZ + x // NX * NZ + z


def shift(value, dx=0, dy=0, dz=0, dc=0):
    size = NX * NH
    pairs = [
        (index(x, y, z, c), index((x + dx) % size, (y + dy) % NY, (z + dz) % NZ, (c + dc) % NC))
        for x in range(size)
        for y in range(NY)
        for z in range(NZ)
        for c in range(NC)
    ]
    return lax.ppermute(value, ("dp", "blk"), pairs)


def by_core(value, dx=0, dy=0, dz=0):
    size = NX * NH
    pairs = []
    for x in range(size):
        for y in range(NY):
            for z in range(NZ):
                for c, way in ((0, 1), (1, -1)):
                    target = ((x + way * dx) % size, (y + way * dy) % NY, (z + way * dz) % NZ, c)
                    pairs.append((index(x, y, z, c), index(*target)))
    return lax.ppermute(value, ("dp", "blk"), pairs)


def swap(value, dy=0):
    pairs = [
        (index(x, y, z, c), index(x ^ 1, (y + dy) % NY, z, c))
        for x in range(NX * NH)
        for y in range(NY)
        for z in range(NZ)
        for c in range(NC)
    ]
    return lax.ppermute(value, ("dp", "blk"), pairs)


def dot(a, b):
    return jnp.dot(a, b, preferred_element_type=jnp.float32)


def space(kind):
    return pl.BlockSpec(memory_space=kind)


def pieces_kernel(columns_ref, source, out, held, arrived, left):
    moves = []
    for k in range(held.shape[0]):
        column = pl.multiple_of(columns_ref[k], 128)
        get = source.at[:, pl.ds(column, held.shape[2])]
        moves.append(
            (
                pltpu.make_async_copy(get, held.at[k], arrived.at[k]),
                pltpu.make_async_copy(held.at[k], out.at[k], left.at[k]),
            )
        )
    for get, put in moves:
        get.start()
    for get, put in moves:
        get.wait()
        put.start()
    for get, put in moves:
        put.wait()


def pieces(columns, activations, depth):
    tokens, count = activations.shape[0], columns.shape[0]
    shape = (count, tokens, depth)
    return pl.pallas_call(
        pieces_kernel,
        out_shape=jax.ShapeDtypeStruct(shape, activations.dtype),
        in_specs=[space(pltpu.SMEM), space(pltpu.HBM)],
        out_specs=space(pltpu.HBM),
        scratch_shapes=[
            pltpu.VMEM(shape, activations.dtype),
            pltpu.SemaphoreType.DMA((count,)),
            pltpu.SemaphoreType.DMA((count,)),
        ],
        compiler_params=pltpu.CompilerParams(vmem_limit_bytes=VMEM),
        cost_estimate=pl.CostEstimate(flops=0, bytes_accessed=2**22, transcendentals=0),
    )(columns, activations)


def product_kernel(moves, layout, *refs):
    table, sources, refs = refs[0], refs[1 : 1 + layout[0]], refs[1 + layout[0] :]
    parts, refs = refs[: sum(layout[1])], refs[sum(layout[1]) :]
    before, (out, rows, panels, semaphore) = refs[:-4], refs[-4:]
    pairs = moves(table, sources, rows)
    for_rows = [pltpu.make_async_copy(*pair, semaphore.at[n]) for n, pair in enumerate(pairs)]
    for_panels, at = [], 0
    for k, count in enumerate(layout[1]):
        filled, copies = 0, []
        for part in parts[at : at + count]:
            target = panels.at[k, pl.ds(filled, part.shape[0])]
            number = len(pairs) + at + len(copies)
            copies.append(pltpu.make_async_copy(part, target, semaphore.at[number]))
            filled += part.shape[0]
        at += count
        for_panels.append(copies)
    if before:
        carry = pltpu.make_async_copy(before[0], out, semaphore.at[len(pairs) + len(parts)])
        carry.start()
    for copy in for_rows + sum(for_panels, []):
        copy.start()
    for copy in for_rows:
        copy.wait()
    for k, copies in enumerate(for_panels):
        for copy in copies:
            copy.wait()
        term = dot(rows[k], panels[k])
        if before and not k:
            carry.wait()
        if k or before:
            out[...] += term
        else:
            out[...] = term


def product(moves, count, table, sources, panels, before=None, followed_by=0, grant=VMEM):
    tokens, blocks = EXAMPLES * TOK, len(panels)
    depth, width = panels[0][0].shape[0] if len(panels[0]) == 1 else sum(
        part.shape[0] for part in panels[0]
    ), panels[0][0].shape[1]
    parts = sum(panels, [])
    layout = (len(sources), [len(panel) for panel in panels])
    extra = [] if before is None else [before]
    return pl.pallas_call(
        lambda *refs: product_kernel(moves, layout, *refs),
        out_shape=jax.ShapeDtypeStruct((tokens, width), jnp.float32),
        in_specs=[space(pltpu.SMEM)]
        + [space(pl.ANY)] * (len(sources) + len(parts) + len(extra)),
        out_specs=space(pltpu.VMEM),
        scratch_shapes=[
            pltpu.VMEM((blocks, tokens, depth), jnp.bfloat16),
            pltpu.VMEM((blocks, depth, width), jnp.bfloat16),
            pltpu.SemaphoreType.DMA((count + len(parts) + len(extra),)),
        ],
        compiler_params=pltpu.CompilerParams(vmem_limit_bytes=grant),
        cost_estimate=pl.CostEstimate(
            flops=2 * tokens * width * blocks * depth + followed_by,
            bytes_accessed=2**22,
            transcendentals=0,
        ),
    )(table, *sources, *parts, *extra)


def near_moves(table, sources, rows):
    near, away = sources
    return [
        (near, rows.at[pl.ds(table[0] * SPLIT, SPLIT)]),
        (away, rows.at[pl.ds((1 - table[0]) * SPLIT, SPLIT)]),
    ]


def rest_moves(table, sources, rows):
    return [(sources[0], rows)]


def own_moves(table, sources, rows):
    return [
        (sources[0].at[:, pl.ds(pl.multiple_of(table[k], 128), rows.shape[2])], rows.at[k])
        for k in range(rows.shape[0])
    ]


def squares_kernel(where_ref, out_rows, *refs):
    blocks = out_rows.shape[0]
    in_rows, refs = refs[:blocks], refs[blocks:]
    totals, (inner, semaphore) = refs[:2], refs[2:]
    copies = [
        pltpu.make_async_copy(in_rows[k], inner.at[k], semaphore.at[k]) for k in range(blocks)
    ]
    for copy in copies:
        copy.start()
    for copy in copies:
        copy.wait()

    @pl.loop(0, inner.shape[2] // TILE)
    def _(n):
        columns = pl.ds(pl.multiple_of(n * TILE, TILE), TILE)
        for part, total_ref in enumerate(totals):
            total = None
            for k in range(blocks):
                at, half = where_ref[k] + where_ref[2 * blocks + part], where_ref[blocks + k]
                for example in range(EXAMPLES):
                    tokens = pl.ds(example * TOK, TOK)
                    rotated = dot(out_rows[at, half, :, tokens], inner[k, tokens, columns])
                    squared = rotated * rotated
                    total = squared if total is None else total + squared
            total_ref[:, columns] = total


TILE = 256


def sums_of_squares(where, out_rows, in_rows):
    rows, tokens = out_rows.shape[2:]
    width, blocks = in_rows[0].shape[1], len(in_rows)
    return pl.pallas_call(
        squares_kernel,
        out_shape=[jax.ShapeDtypeStruct((rows, width), jnp.float32)] * 2,
        in_specs=[space(pltpu.SMEM), space(pltpu.VMEM)] + [space(pl.ANY)] * blocks,
        out_specs=[space(pltpu.VMEM)] * 2,
        scratch_shapes=[
            pltpu.VMEM((blocks, tokens, width), jnp.bfloat16),
            pltpu.SemaphoreType.DMA((blocks,)),
        ],
        compiler_params=pltpu.CompilerParams(vmem_limit_bytes=TAIL_VMEM),
        cost_estimate=pl.CostEstimate(
            flops=4 * rows * width * blocks * tokens,
            bytes_accessed=out_rows.size * 2 + rows * width * 8,
            transcendentals=0,
        ),
    )(where, out_rows, *in_rows)


def transposed(block):
    pairs = []
    for sx in range(NX):
        for sy in range(NY):
            for sc in range(NC):
                for t in range(NX * NY * NC):
                    source = ((sx * NY + sy) * NC + sc) * NH * NZ + t
                    target = (t // NC * NC + sc) * NH * NZ + sx * NZ + sy * NC + t % NC
                    pairs.append((source, target))
    return lax.ppermute(block, ("dp", "blk"), pairs)


def on_device(activations, out_grads, basis_in, basis_out):
    d, b = lax.axis_index("dp"), lax.axis_index("blk")
    core, y, x = d % NC, (d // NC) % NY, d // (NC * NY)
    parity = b % 2
    scale = 1.0 / float(EXAMPLES * NX * NY * NC)
    depth = basis_in.shape[0]
    mirror = 1 - 2 * core
    spots = [((y + mirror * dy) % NY) * NC + (core + dc) % NC for dy, dc in BLOCKS]
    half = len(BLOCKS)

    table = jnp.stack(spots).astype(jnp.int32)
    give = (half * (1 - x) + table) * depth
    keep = ((half * x + table) * depth).astype(jnp.int32)
    first, own_other = by_core(basis_in, dy=1), shift(basis_in, dc=1)
    near = lax.dynamic_slice_in_dim(give, parity * SPLIT, SPLIT)
    near = pieces(near.astype(jnp.int32), activations, depth)
    rest = pieces(give[2 * SPLIT :].astype(jnp.int32), activations, depth)
    block = transposed(dot(out_grads, basis_out).astype(jnp.bfloat16).T)
    near, block = lax.optimization_barrier((near, block))
    near = by_core(near, dx=1)
    first, again = lax.optimization_barrier((first, basis_in))
    second, far = by_core(again, dy=NY - 1), by_core(first, dy=1)
    near, rest, first = lax.optimization_barrier((near, rest, first))
    first_other = shift(first, dc=1)
    rest, away = by_core(rest, dx=1), by_core(near, dz=1)

    other = shift(block, dx=NX)
    out_rows = lax.all_gather(
        jnp.stack([block, other]),
        "blk",
        axis=0,
        axis_index_groups=[[h * NZ + z for z in range(NZ)] for h in range(NH)],
    )
    where = jnp.stack(
        [(y + dy) % NY * NC for dx, dy in ORDER]
        + [(x + dx + b // NZ) % 2 for dx, dy in ORDER]
        + [core, 1 - core]
    ).astype(jnp.int32)

    panels = [[panel] for panel in (basis_in, own_other, first, first_other)]
    mine = product(own_moves, 2 * SPLIT, keep[: 2 * SPLIT], (activations,), panels)
    mine, second = lax.optimization_barrier((mine, second))
    for panel in (second, far):
        panels += [[panel], [shift(panel, dc=1)]]
    parity = parity.reshape(1).astype(jnp.int32)
    partial = product(
        near_moves, 2, parity, (near, away), panels[: 2 * SPLIT], None, 0, OWN_VMEM
    )
    partial = product(
        rest_moves, 1, parity, (rest,), panels[2 * SPLIT :], partial, FOLLOWED, TAIL_VMEM
    )
    arrived = swap((partial * FACTOR).astype(jnp.float16))
    total = product(
        own_moves, 2 * SPLIT, keep[2 * SPLIT :], (activations,), panels[2 * SPLIT :], mine, 0, OWN_VMEM
    )
    proj_in = (total + arrived.astype(jnp.float32) * (1.0 / FACTOR)).astype(jnp.bfloat16)

    p_left, p_right, p_far = shift(proj_in, dy=1), shift(proj_in, dy=3), shift(proj_in, dy=2)
    p_across = swap(proj_in)
    px_left, px_right = shift(p_across, dy=1), shift(p_across, dy=3)
    px_far = swap(p_far)
    kept, given = sums_of_squares(
        where,
        out_rows,
        (proj_in, p_left, p_right, p_across, p_far, px_left, px_right, px_far),
    )
    return (kept + shift(given, dc=1)) * jnp.float32(scale)


def solution(mesh):
    return jax.shard_map(
        on_device,
        mesh=mesh,
        in_specs=(P("dp", None), P("dp", None), P("dp", "blk"), P(None, "blk")),
        out_specs=P("dp", "blk"),
        check_vma=False,
    )
```
